32 devices in a mesh: row: 8 (over y, x, core), col: 4 (over z).
Axes of the slice: x: 2, y: 2, z: 4, core: 2. Of those that a mesh axis runs over, the one named last changes fastest.
Arguments:
- test_kernel: float32 [16384, 2048], P('row', 'col'), may hold values from -6 to 6
- first_panel: float32 [16384, 512], P('row', 'col'), may hold values from -0.25 to 0.25
- second_panel: float32 [16384, 512], P('row', 'col'), may hold values from -0.25 to 0.25
- first_inverse: float32 [512, 512], replicated, may hold values from -0.15 to 1.5, as said below
- second_inverse: float32 [512, 512], replicated, may hold values from -0.15 to 1.5, as said below
Outputs:
- solution: float32 [16384, 2048], P('row', 'col')
The draws below stay inside these ranges and needn't reach their ends.
Inputs may be any that keep to these rules, and one draw needn't show every extreme that they name: `first_inverse`: lower triangular: zeros above the diagonal, diagonal entries positive. `second_inverse`: lower triangular: zeros above the diagonal, diagonal entries positive.
All inputs are finite; a program needn't handle non-finite values.
Results may differ from the reference program's by a relative error of at most 0.000075.
Values sent between devices are 32-bit elements; how exact they have to be, the bound alone decides.
No kernel may reach another device: no remote copies, remote signals or barrier semaphores. Data moves between devices by JAX's collectives and lax.ppermute only.
A program may use at most 64 MiB of HBM per device.

```python
import jax
import jax.numpy as jnp
from jax import lax

B = 512
ROWS_DEV = 2048
ROWS = 16384
TESTS = 2048


def triangle_draw(key, which):
    base = jax.random.fold_in(key, which)
    key_diagonal = jax.random.fold_in(base, 1)
    key_lower = jax.random.fold_in(base, 2)
    diagonal_part = jax.random.uniform(key_diagonal, (B,), jnp.float32, 0.6, 1.4)
    lower_part = jnp.clip(0.03 * jax.random.normal(key_lower, (B, B), jnp.float32), -0.15, 0.15)
    row_index = jnp.arange(B)[:, None]
    column_index = jnp.arange(B)[None, :]
    strict_lower = jnp.where(row_index > column_index, lower_part, 0.0)
    return strict_lower + jnp.where(row_index == column_index, diagonal_part[:, None], 0.0)


def draw_first_inverse(key, part):
    return triangle_draw(key, 11)


def draw_second_inverse(key, part):
    return triangle_draw(key, 23)


def block_scale(key, extent, pieces, low, top_value):
    def one(dim, parts):
        heights = jax.random.uniform(jax.random.fold_in(jax.random.fold_in(key, 6), dim), (parts,), jnp.float32, low / len(pieces), top_value / len(pieces))
        return jnp.repeat(jnp.exp(heights), extent[dim] // parts).reshape((-1,) + (1,) * (len(extent) - dim - 1))

    gain = one(*pieces[0])
    for cut in pieces[1:]:
        gain = gain * one(*cut)
    return gain


def centred(own_key, dims, spread, reach, pieces=(), dtype=jnp.bfloat16):
    entries = jax.random.normal(own_key, dims, jnp.float32) * spread
    if len(pieces) > 0:
        entries = block_scale(own_key, dims, pieces, -0.22, 0.18) * entries
    return jnp.clip(entries, min=-reach, max=reach).astype(dtype)


def setup_inputs(seed: int = 0) -> dict:
    streams_of = jax.random.split(jax.random.key(seed), 6)
    test_kernel = centred(streams_of[0], (ROWS, TESTS), 1.0, 6.0, ((0, 8), (1, 4)), jnp.float32)
    first_panel = centred(streams_of[1], (ROWS, B), B ** -0.5, 0.25, ((0, 8), (1, 4)), jnp.float32)
    second_panel = centred(streams_of[2], (ROWS, B), B ** -0.5, 0.25, ((0, 8), (1, 4)), jnp.float32)
    first_inverse = draw_first_inverse(jax.random.fold_in(streams_of[5], 71), 0)
    second_inverse = draw_second_inverse(jax.random.fold_in(streams_of[5], 71), 0)
    return {"test_kernel": test_kernel, "first_panel": first_panel, "second_panel": second_panel, "first_inverse": first_inverse, "second_inverse": second_inverse}


def product(left, right):
    return jnp.dot(left, right, precision=lax.Precision.HIGHEST, preferred_element_type=jnp.float32)


def reference(test_kernel, first_panel, second_panel, first_inverse, second_inverse):
    first_solved = product(first_inverse, test_kernel[:B])
    partial_value = test_kernel - product(first_panel, first_solved)
    second_solved = product(second_inverse, partial_value[ROWS_DEV:ROWS_DEV + B])
    final = partial_value - product(second_panel, second_solved)
    final = final.at[:B].set(first_solved)
    final = final.at[ROWS_DEV:ROWS_DEV + B].set(second_solved)
    return final
```

```python
import jax
import jax.numpy as jnp
from jax import lax
from jax.sharding import PartitionSpec as P

PARTS = 8
RAW_PARTS = 4


def product(left, right):
    return jnp.dot(left, right, precision=lax.Precision.HIGH, preferred_element_type=jnp.float32)


def broadcast(value, axis, source):
    kept = jnp.where(lax.axis_index(axis) == source, value, 0).astype(value.dtype)
    return lax.psum(kept, axis)


def general(test_kernel, first_panel, second_panel, first_inverse, second_inverse):
    block = first_inverse.shape[0]
    position = lax.axis_index("row")
    first_rows = broadcast(test_kernel[:block], "row", 0)
    first_solved = product(first_inverse, first_rows)
    partial_value = test_kernel - product(lax.all_gather(first_panel, "col", axis=1, tiled=True), first_solved)
    second_rows = broadcast(partial_value[:block], "row", 1)
    second_solved = product(second_inverse, second_rows)
    final = partial_value - product(lax.all_gather(second_panel, "col", axis=1, tiled=True), second_solved)
    leading_final = jnp.where(
        position == 0, first_solved, jnp.where(position == 1, second_solved, final[:block])
    )
    return final.at[:block].set(leading_final)


AXES = ("row", "col")
ROWS, COLS = 8, 4
END_MID = ((0, 1), (3, 2))
MID_MID = ((1, 2), (2, 1))
MID_END = ((1, 0), (2, 3))


def along_col(value, pairs, rows):
    return lax.ppermute(value, AXES, [(r * COLS + a, r * COLS + b) for r in rows for a, b in pairs])


def along_row(value, pairs, cols):
    return lax.ppermute(value, AXES, [(a * COLS + c, b * COLS + c) for a, b in pairs for c in cols])


ALL_COLS = (0, 1, 2, 3)
MID_COLS = (1, 2)
SWAP = tuple((r, r ^ 1) for r in range(ROWS))


def spread(value, cols):
    row = lax.axis_index("row")
    even = row % 2 == 0
    half = value.shape[0] // 2
    mine = jnp.where(even, value[:half], value[half:])
    near = along_row(mine, ((0, 2), (1, 5)), cols)
    mine = jnp.where((row == 2) | (row == 5), near, mine)
    far = along_row(mine, ((2, 6), (5, 7), (0, 4), (1, 3)), cols)
    mine = jnp.where((row == 3) | (row == 4) | (row >= 6), far, mine)
    other = along_row(mine, SWAP, cols)
    return jnp.concatenate([jnp.where(even, mine, other), jnp.where(even, other, mine)], axis=0)


def four(test_kernel, first_panel, second_panel, first_inverse, second_inverse):
    block = first_inverse.shape[0]
    rows, width = test_kernel.shape
    slab = first_panel.shape[1]
    part = rows // PARTS
    row, col = lax.axis_index("row"), lax.axis_index("col")
    end = (col == 0) | (col == COLS - 1)
    left = col < COLS // 2
    every = range(ROWS)

    corner = first_panel[:block]
    one = (1,)
    corner_end = along_col(corner, END_MID, one)
    corner_mid = along_col(corner, MID_MID, one)
    corner_far = along_col(corner_end, MID_MID, one)
    corner_c = along_col(corner, MID_END, one)
    corner_c2 = along_col(corner_mid, MID_END, one)
    corner_c3 = along_col(corner_far, MID_END, one)
    corner_all = jnp.concatenate(
        [
            jnp.where(end, corner, corner_end),
            jnp.where(end, corner_c, corner),
            jnp.where(end, corner_c2, corner_mid),
            jnp.where(end, corner_c3, corner_far),
        ],
        axis=1,
    )

    def relative(solved):
        pieces = solved.reshape(COLS, block // COLS, width)
        return jnp.where(left, pieces, pieces[::-1])

    top = test_kernel[:block]
    top_end = along_col(top, END_MID, (0, 1))

    def solve(own_top, cols):
        first = jnp.where(row == 1, along_row(own_top, ((0, 1),), cols), own_top)
        first_solved = product(first_inverse, first)
        value = own_top - product(corner_all, relative(first_solved).reshape(block, width))
        second_solved = product(second_inverse, value)
        second_half = along_row(second_solved[: block // 2], ((1, 0),), cols)
        second_held = second_solved.at[: block // 2].set(
            jnp.where(row == 0, second_half, second_solved[: block // 2])
        )
        return first_solved, second_held

    def stacked(first_solved, second_solved):
        return jnp.concatenate([relative(first_solved), relative(second_solved)], axis=1).reshape(
            2 * block, width
        )

    first_end, second_end = solve(top_end, MID_COLS)
    first_end, second_end = spread(first_end, MID_COLS), spread(second_end, MID_COLS)
    solved_end = stacked(first_end, second_end)
    first_own, second_own = solve(top, ALL_COLS)
    first_own, second_own = spread(first_own, ALL_COLS), spread(second_own, ALL_COLS)
    solved_own = stacked(first_own, second_own)

    out = []
    for index in range(PARTS):
        low, high = index * part, (index + 1) * part
        members = every if low >= block else range(2, ROWS)
        own = jnp.concatenate([first_panel[low:high], second_panel[low:high]], axis=1)
        from_end = along_col(own, END_MID, members)
        from_mid = along_col(own, MID_MID, members)
        from_far = along_col(from_end, MID_MID, members)
        if index < RAW_PARTS:
            near = along_col(own, MID_END, members)
            mid = along_col(from_mid, MID_END, members)
            far = along_col(from_far, MID_END, members)
            panels = jnp.concatenate(
                [
                    jnp.where(end, own, from_end),
                    jnp.where(end, near, own),
                    jnp.where(end, mid, from_mid),
                    jnp.where(end, far, from_far),
                ],
                axis=1,
            )
            update = product(panels, solved_own)
        else:
            panels = jnp.concatenate([from_end, own, from_mid, from_far], axis=1)
            sent = along_col(product(panels, solved_end), MID_END, members)
            update = jnp.where(end, sent, product(panels, solved_own))
        piece = test_kernel[low:high] - update
        if low < block:
            piece = jnp.where(
                row == 0, first_own[low:high], jnp.where(row == 1, second_own[low:high], piece)
            )
        out.append(piece)
    return jnp.concatenate(out, axis=0)


def solution(mesh):
    in_specs = (P("row", "col"), P("row", "col"), P("row", "col"), P(), P())
    out_specs = P("row", "col")
    body = four if dict(mesh.shape) == {"row": ROWS, "col": COLS} else general
    return jax.shard_map(body, mesh=mesh, in_specs=in_specs, out_specs=out_specs, check_vma=False)
```

```python
import jax
import jax.numpy as jnp
from jax import lax
from jax.sharding import PartitionSpec as P


def product(left, right):
    return jnp.dot(left, right, precision=lax.Precision.HIGH, preferred_element_type=jnp.float32)


def broadcast(value, axis, source):
    kept = jnp.where(lax.axis_index(axis) == source, value, 0).astype(value.dtype)
    return lax.psum(kept, axis)


def general(test_kernel, first_panel, second_panel, first_inverse, second_inverse):
    block = first_inverse.shape[0]
    position = lax.axis_index("row")
    first_rows = broadcast(test_kernel[:block], "row", 0)
    first_solved = product(first_inverse, first_rows)
    partial_value = test_kernel - product(lax.all_gather(first_panel, "col", axis=1, tiled=True), first_solved)
    second_rows = broadcast(partial_value[:block], "row", 1)
    second_solved = product(second_inverse, second_rows)
    final = partial_value - product(lax.all_gather(second_panel, "col", axis=1, tiled=True), second_solved)
    leading_final = jnp.where(
        position == 0, first_solved, jnp.where(position == 1, second_solved, final[:block])
    )
    return final.at[:block].set(leading_final)


AXES = ("row", "col")
ROWS, COLS = 8, 4
END_MID = ((0, 1), (3, 2))
MID_MID = ((1, 2), (2, 1))
MID_END = ((1, 0), (2, 3))


def along_col(value, pairs, rows):
    return lax.ppermute(value, AXES, [(r * COLS + a, r * COLS + b) for r in rows for a, b in pairs])


def along_row(value, pairs, cols):
    return lax.ppermute(value, AXES, [(a * COLS + c, b * COLS + c) for a, b in pairs for c in cols])


ALL_COLS = (0, 1, 2, 3)
MID_COLS = (1, 2)
SWAP = tuple((r, r ^ 1) for r in range(ROWS))


def four(test_kernel, first_panel, second_panel, first_inverse, second_inverse):
    block = first_inverse.shape[0]
    rows, width = test_kernel.shape
    raw = 2 * block
    bounds = [(2 * block, 3 * block), (3 * block, 4 * block)]
    row, col = lax.axis_index("row"), lax.axis_index("col")
    end = (col == 0) | (col == COLS - 1)
    left = col < COLS // 2
    every = range(ROWS)
    tied = lax.optimization_barrier
    even = row % 2 == 0
    half = block // 2

    def pieces(solved):
        return solved.reshape(COLS, block // COLS, width)

    def both(low, high):
        return jnp.concatenate([first_panel[low:high], second_panel[low:high]], axis=1)

    def near(mine):
        got = along_row(mine, ((0, 2), (1, 5)), ALL_COLS)
        return jnp.where((row == 2) | (row == 5), got, mine)

    def far(mine):
        got = along_row(mine, ((2, 6), (5, 7), (0, 4), (1, 3)), ALL_COLS)
        return jnp.where((row == 3) | (row == 4) | (row >= 6), got, mine)

    def whole(mine):
        other = along_row(mine, SWAP, ALL_COLS)
        low, high = jnp.where(even, mine, other), jnp.where(even, other, mine)
        first = jnp.concatenate([low[:half], high[:half]], axis=0)
        second = jnp.concatenate([low[half:], high[half:]], axis=0)
        return jnp.concatenate([pieces(first), pieces(second)], axis=1)

    most, corner_rows = range(2, ROWS), (0, 1)
    corner = first_panel[:block]
    one = (1,)
    corner_swap = along_col(corner, END_MID + MID_END, one)
    corner_mid = along_col(corner, MID_MID, one)
    raw_own = both(0, raw)
    raw_swap = along_col(raw_own, END_MID + MID_END, most)
    raw_mid = along_col(raw_own, MID_MID, most)
    corner_far = along_col(corner_swap, MID_MID, one)
    corner_c = along_col(corner_mid, MID_END, one)
    corner_cc = along_col(corner_far, MID_END, one)
    corners = jnp.concatenate(
        [
            jnp.where(end, corner, corner_swap),
            jnp.where(end, corner_swap, corner),
            jnp.where(end, corner_c, corner_mid),
            jnp.where(end, corner_cc, corner_far),
        ],
        axis=1,
    )

    top = test_kernel[:block]
    first = product(first_inverse, top)
    first = jnp.where(row == 1, along_row(first, ((0, 1),), ALL_COLS), first)
    mine_one = far(near(jnp.where(even, first[:half], first[half:])))
    own = [both(low, high) for low, high in bounds]
    few_own = both(block, raw)

    corners, mine_one, own, few_own, raw_swap, raw_mid = tied(
        (corners, mine_one, own, few_own, raw_swap, raw_mid)
    )
    raw_far = along_col(raw_swap, MID_MID, most)
    raw_c = along_col(raw_mid, MID_END, most)
    from_end = [along_col(own[0], END_MID, every)]
    hop_one = along_col(mine_one, END_MID, every)
    few_swap = along_col(few_own, END_MID + MID_END, corner_rows)
    few_mid = along_col(few_own, MID_MID, corner_rows)
    slices = pieces(first)
    slices = jnp.where(left, slices, slices[::-1]).reshape(block, width)
    second = product(second_inverse, top - product(corners, slices))
    upper = along_row(second[:half], ((1, 0),), ALL_COLS)
    mine_two = near(jnp.where(even, upper, second[half:]))

    mine_two, few_swap, few_mid, own = tied((mine_two, few_swap, few_mid, own))
    few_far = along_col(few_swap, MID_MID, corner_rows)
    few_c = along_col(few_mid, MID_END, corner_rows)
    from_mid = [along_col(own[0], MID_MID, every)]
    mine_two = far(mine_two)

    mine_two, raw_far, raw_c, from_end[0], hop_one, few_far, few_c, own = tied(
        (mine_two, raw_far, raw_c, from_end[0], hop_one, few_far, few_c, own)
    )
    hop_two = along_col(mine_two, END_MID, every)
    raw_cc = along_col(raw_far, MID_END, most)
    few_cc = along_col(few_far, MID_END, corner_rows)
    from_far = [along_col(from_end[0], MID_MID, every)]
    from_mid.append(along_col(own[1], MID_MID, every))
    solved_own = whole(jnp.concatenate([mine_one, mine_two], axis=0))

    hop_two, solved_own, own = tied((hop_two, solved_own, own))
    from_end.append(along_col(own[1], END_MID, every))
    solved_end = whole(jnp.concatenate([hop_one, hop_two], axis=0))
    solved_end = jnp.where(left, solved_end, solved_end[::-1]).reshape(2 * block, width)
    solved_turned = jnp.where(left, solved_own, solved_own[::-1]).reshape(2 * block, width)

    solved_end, solved_turned, from_end[1], from_far[0], from_mid[0] = tied(
        (solved_end, solved_turned, from_end[1], from_far[0], from_mid[0])
    )
    from_far.append(along_col(from_end[1], MID_MID, every))

    def panels(i):
        return jnp.concatenate([from_end[i], own[i], from_mid[i], from_far[i]], axis=1)

    sent = product(panels(0), solved_end)
    sent, raw_cc, few_cc = tied((sent, raw_cc, few_cc))
    returned = [along_col(sent, MID_END, every)]

    def raw_panels(own, swap, mid, far, c, cc):
        return jnp.concatenate(
            [
                jnp.where(end, own, swap),
                jnp.where(end, swap, own),
                jnp.where(end, c, mid),
                jnp.where(end, cc, far),
            ],
            axis=1,
        )

    few_panels = raw_panels(few_own, few_swap, few_mid, few_far, few_c, few_cc)
    most_panels = raw_panels(raw_own, raw_swap, raw_mid, raw_far, raw_c, raw_cc)
    first_own = solved_own[:, : block // COLS].reshape(block, width)
    second_own = solved_own[:, block // COLS :].reshape(block, width)
    lead = test_kernel[:block] - product(most_panels[:block], solved_turned)
    lead = jnp.where(row == 0, first_own, jnp.where(row == 1, second_own, lead))
    lower = jnp.where(row < 2, few_panels, most_panels[block:])
    out = [lead, test_kernel[block:raw] - product(lower, solved_turned)]
    mine = [test_kernel[low:high] - product(panels(i), solved_turned) for i, (low, high) in enumerate(bounds)]
    returned.append(along_col(product(panels(1), solved_end), MID_END, every))
    for i, (low, high) in enumerate(bounds):
        out.append(jnp.where(end, test_kernel[low:high] - returned[i], mine[i]))
    return jnp.concatenate(out, axis=0)


def solution(mesh):
    in_specs = (P("row", "col"), P("row", "col"), P("row", "col"), P(), P())
    out_specs = P("row", "col")
    body = four if dict(mesh.shape) == {"row": ROWS, "col": COLS} else general
    return jax.shard_map(body, mesh=mesh, in_specs=in_specs, out_specs=out_specs, check_vma=False)
```

```python
import functools

import jax
import jax.numpy as jnp
from jax import lax
from jax.experimental import pallas as pl
from jax.experimental.pallas import tpu as pltpu
from jax.sharding import PartitionSpec as P

STAGE_FLOPS = 8*10**10


def product(left, right):
    return jnp.dot(left, right, precision=lax.Precision.HIGH, preferred_element_type=jnp.float32)


def broadcast(value, axis, source):
    kept = jnp.where(lax.axis_index(axis) == source, value, 0).astype(value.dtype)
    return lax.psum(kept, axis)


def general(test_kernel, first_panel, second_panel, first_inverse, second_inverse):
    block = first_inverse.shape[0]
    position = lax.axis_index("row")
    first_rows = broadcast(test_kernel[:block], "row", 0)
    first_solved = product(first_inverse, first_rows)
    partial_value = test_kernel - product(lax.all_gather(first_panel, "col", axis=1, tiled=True), first_solved)
    second_rows = broadcast(partial_value[:block], "row", 1)
    second_solved = product(second_inverse, second_rows)
    final = partial_value - product(lax.all_gather(second_panel, "col", axis=1, tiled=True), second_solved)
    leading_final = jnp.where(
        position == 0, first_solved, jnp.where(position == 1, second_solved, final[:block])
    )
    return final.at[:block].set(leading_final)


AXES = ("row", "col")
ROWS, COLS = 8, 4
END_MID = ((0, 1), (3, 2))
MID_MID = ((1, 2), (2, 1))
MID_END = ((1, 0), (2, 3))


def along_col(value, pairs, rows):
    return lax.ppermute(value, AXES, [(r * COLS + a, r * COLS + b) for r in rows for a, b in pairs])


def along_row(value, pairs, cols):
    return lax.ppermute(value, AXES, [(a * COLS + c, b * COLS + c) for a, b in pairs for c in cols])


ALL_COLS = (0, 1, 2, 3)
MID_COLS = (1, 2)
SWAP = tuple((r, r ^ 1) for r in range(ROWS))


def split(value):
    high = value.astype(jnp.bfloat16)
    return high, (value - high.astype(jnp.float32)).astype(jnp.bfloat16)


def three_pass(left, right):
    def one(a, b):
        return jnp.dot(a, b, preferred_element_type=jnp.float32)

    return one(left[0], right[0]) + (one(left[0], right[1]) + one(left[1], right[0]))


TILE = 256
VMEM_BYTES = 40 * 2**20
SMEM = pl.BlockSpec(memory_space=pltpu.SMEM)


def halves(place, held, other):
    a, b = held[...], other[...]
    return jnp.where(place[0] == 1, a, b), jnp.where(place[0] == 1, b, a)


def solved_tile(place, tops, inverses, corner):
    low, high = halves(place, *tops)
    half = low.shape[0] // 2
    first_top = jnp.concatenate([low[:half], high[:half]], axis=0)
    second_top = jnp.concatenate([low[half:], high[half:]], axis=0)
    slab = first_top.shape[0] // COLS

    def turned(solved):
        pieces = [solved[k * slab : (k + 1) * slab] for k in range(COLS)]
        return [jnp.where(place[1] == 1, pieces[k], pieces[COLS - 1 - k]) for k in range(COLS)]

    first_high, first_low, second_high, second_low = (ref[...] for ref in inverses)
    first = turned(three_pass((first_high, first_low), split(first_top)))
    value = second_top - three_pass(corner, split(jnp.concatenate(first, axis=0)))
    second = turned(three_pass((second_high, second_low), split(value)))
    return jnp.concatenate([p for pair in zip(first, second) for p in pair], axis=0)


def split_kernel(one, two, *outs):
    outs[0][...], outs[1][...] = split(one[...])
    outs[2][...], outs[3][...] = split(two[...])


def split_inverses(one, two):
    return pl.pallas_call(
        split_kernel, out_shape=[jax.ShapeDtypeStruct(one.shape, jnp.bfloat16)] * 4
    )(one, two)


def multiply_kernel(place, *refs):
    inverses, corner, out = refs[2:6], refs[6:8], refs[-1]
    solved = solved_tile(place, refs[:2], inverses, (corner[0][...], corner[1][...]))
    own, near_end, both = refs[8:11]
    panels = jnp.concatenate([near_end[...], own[...], both[...]], axis=1)
    out[...] = three_pass(split(panels), split(solved))


def own_kernel(place, *refs):
    held, other, inverses, (out, high, low) = refs[2], refs[3], refs[4:8], refs[8:]

    @pl.when(pl.program_id(0) == 0)
    def _():
        high[...], low[...] = split(jnp.concatenate(halves(place, held, other), axis=0))

    out[...] = solved_tile(place, refs[:2], inverses, (high[...], low[...]))


def fixed(value):
    return pl.BlockSpec(value.shape, lambda j: (0, 0))


def solve_and_multiply(place, held, other, inverses, corner, panels):
    width, rows = held.shape[1], panels[0].shape[0]
    tops = pl.BlockSpec((held.shape[0], TILE), lambda j: (0, j))
    fixed_ones = (*inverses, *corner, *panels)
    return pl.pallas_call(
        multiply_kernel,
        grid=(width // TILE,),
        out_shape=jax.ShapeDtypeStruct((rows, width), jnp.float32),
        in_specs=[SMEM, tops, tops] + [fixed(v) for v in fixed_ones],
        out_specs=pl.BlockSpec((rows, TILE), lambda j: (0, j)),
        compiler_params=pltpu.CompilerParams(vmem_limit_bytes=VMEM_BYTES),
        cost_estimate=pl.CostEstimate(flops=4 * 10**9, bytes_accessed=0, transcendentals=0),
    )(place, held, other, *fixed_ones)


def solve_own(place, held, other, inverses):
    block, width = inverses[0].shape[0], held.shape[1]
    tops = pl.BlockSpec((block, TILE), lambda j: (0, j))
    corners = pl.BlockSpec((block // 2, width), lambda j: (2, 0))
    corner = jax.ShapeDtypeStruct((block, block), jnp.bfloat16)
    return pl.pallas_call(
        own_kernel,
        grid=(width // TILE,),
        out_shape=[jax.ShapeDtypeStruct((2 * block, width), jnp.float32), corner, corner],
        in_specs=[SMEM, tops, tops, corners, corners] + [fixed(v) for v in inverses],
        out_specs=[pl.BlockSpec((2 * block, TILE), lambda j: (0, j)), fixed(corner), fixed(corner)],
        compiler_params=pltpu.CompilerParams(vmem_limit_bytes=VMEM_BYTES),
        cost_estimate=pl.CostEstimate(flops=3 * 10**9, bytes_accessed=0, transcendentals=0),
    )(place, held, other, held, other, *inverses)


def update_kernel(sizes, place, top, solved, *refs):
    index = pl.program_id(0)
    out, high, low = refs[-3:]
    groups, last = (refs[:6], refs[6:12]), refs[12:15]
    left, end = place[1] == 1, place[2] == 1

    @pl.when(index == 0)
    def _():
        high[...], low[...] = split(solved[...])

    def apply(panels):
        out[...] = top[...] - three_pass(split(panels), (high[...], low[...]))

    def raw_panels(own, swap, mid, far, c, cc):
        pairs = ((own, swap), (swap, own), (c, mid), (cc, far))
        return jnp.concatenate([jnp.where(end, a[...], b[...]) for a, b in pairs], axis=1)

    @pl.when(index < sizes[0])
    def _():
        apply(raw_panels(*groups[0]))
        slab = solved.shape[0] // (2 * COLS)
        for which in range(2):
            @pl.when(place[3 + which] == 1)
            def _():
                for k in range(TILE // slab):
                    here = index * (TILE // slab) + k
                    here = jnp.where(left, here, COLS - 1 - here)
                    start = pl.multiple_of((2 * here + which) * slab, slab)
                    out[k * slab : (k + 1) * slab] = solved[pl.ds(start, slab)]

    @pl.when((index >= sizes[0]) & (index < sizes[1]))
    def _():
        apply(raw_panels(*groups[1]))

    @pl.when(index >= sizes[1])
    def _():
        own, near_end, both = last
        apply(jnp.concatenate([near_end[...], own[...], both[...]], axis=1))


def update(place, top, solved, groups, last):
    rows, width = top.shape
    ends = [groups[0][0].shape[0] // TILE]
    ends.append(ends[0] + groups[1][0].shape[0] // TILE)
    tiles = rows // TILE

    def rows_of(value, first, past):
        return pl.BlockSpec((TILE, value.shape[1]), lambda i: (jnp.clip(i, first, past - 1) - first, 0))

    specs = [rows_of(v, 0, ends[0]) for v in groups[0]]
    specs += [rows_of(v, ends[0], ends[1]) for v in groups[1]]
    specs += [rows_of(v, ends[1], tiles) for v in last]
    tile = pl.BlockSpec((TILE, width), lambda i: (i, 0))
    return pl.pallas_call(
        functools.partial(update_kernel, ends),
        grid=(tiles,),
        out_shape=jax.ShapeDtypeStruct(top.shape, top.dtype),
        in_specs=[SMEM, tile, pl.BlockSpec(solved.shape, lambda i: (0, 0))] + specs,
        out_specs=tile,
        scratch_shapes=[pltpu.VMEM(solved.shape, jnp.bfloat16)] * 2,
        compiler_params=pltpu.CompilerParams(vmem_limit_bytes=VMEM_BYTES),
        cost_estimate=pl.CostEstimate(flops=7 * 10**9, bytes_accessed=0, transcendentals=0),
    )(place, top, solved, *groups[0], *groups[1], *last)


def finish_kernel(place, top, returned, kept, out):
    out[...] = jnp.where(place[2] == 1, top[...] - returned[...], kept[...])


def finish(place, top, returned, kept):
    rows, width = top.shape
    count = returned.shape[0] // TILE
    first = (rows - returned.shape[0]) // TILE
    tile = pl.BlockSpec((TILE, width), lambda i: (first + i, 0))
    return pl.pallas_call(
        finish_kernel,
        grid=(count,),
        out_shape=jax.ShapeDtypeStruct(top.shape, top.dtype),
        in_specs=[SMEM, tile, pl.BlockSpec((TILE, width), lambda i: (i, 0)), tile],
        out_specs=tile,
        input_output_aliases={3: 0},
        compiler_params=pltpu.CompilerParams(vmem_limit_bytes=VMEM_BYTES),
    )(place, top, returned, kept)


def nothing(*refs):
    pass


def stage(*values):
    anywhere = [pl.BlockSpec(memory_space=pl.ANY)] * len(values)
    return pl.pallas_call(
        nothing,
        out_shape=[jax.ShapeDtypeStruct(v.shape, v.dtype) for v in values],
        in_specs=anywhere,
        out_specs=anywhere,
        input_output_aliases={i: i for i in range(len(values))},
        cost_estimate=pl.CostEstimate(flops=STAGE_FLOPS, bytes_accessed=0, transcendentals=0),
    )(*values)


def four(test_kernel, first_panel, second_panel, first_inverse, second_inverse):
    block = first_inverse.shape[0]
    rows, width = test_kernel.shape
    raw = 3 * block
    half = block // 2
    row, col = lax.axis_index("row"), lax.axis_index("col")
    end = (col == 0) | (col == COLS - 1)
    left = col < COLS // 2
    even = row % 2 == 0
    every, most, one = range(ROWS), range(2, ROWS), (1,)
    both_ways = END_MID + MID_END
    tied = lax.optimization_barrier

    def both(low, high):
        return jnp.concatenate([first_panel[low:high], second_panel[low:high]], axis=1)

    def near(mine):
        got = along_row(mine, ((0, 2), (1, 5)), ALL_COLS)
        return jnp.where((row == 2) | (row == 5), got, mine)

    def far(mine):
        got = along_row(mine, ((2, 6), (5, 7), (0, 4), (1, 3)), ALL_COLS)
        return jnp.where((row == 3) | (row == 4) | (row >= 6), got, mine)

    def ordered(own, swap, mid, far, c, cc):
        return jnp.concatenate(
            [
                jnp.where(end, own, swap),
                jnp.where(end, swap, own),
                jnp.where(end, c, mid),
                jnp.where(end, cc, far),
            ],
            axis=1,
        )

    first_high, first_low, second_high, second_low = split_inverses(first_inverse, second_inverse)
    inverses = (first_high, first_low, second_high, second_low)

    corner = first_panel[:block]
    corner_swap = along_col(corner, both_ways, one)
    corner_mid = along_col(corner, MID_MID, one)
    corner_far = along_col(corner_swap, MID_MID, one)
    corner_c = along_col(corner_mid, MID_END, one)

    lead_own = both(0, block)
    lead_swap = along_col(lead_own, both_ways, most)
    lead_mid = along_col(lead_own, MID_MID, most)
    rest_own = both(block, raw)
    rest_swap = along_col(rest_own, both_ways, every)
    rest_mid = along_col(rest_own, MID_MID, every)

    top = test_kernel[:block]
    given = along_row(jnp.where(even, top[half:], top[:half]), ((0, 1), (1, 0)), ALL_COLS)
    mine = jnp.where(
        even,
        jnp.concatenate([top[:half], given], axis=0),
        jnp.concatenate([given, top[half:]], axis=0),
    )
    mine, lead_swap, lead_mid = tied((near(mine), lead_swap, lead_mid))
    lead_swap, lead_mid = stage(lead_swap, lead_mid)
    lead_c = along_col(lead_mid, MID_END, most)
    lead_far = along_col(lead_swap, MID_MID, most)
    mine = far(mine)

    mine, rest_swap, rest_mid = tied((mine, rest_swap, rest_mid))
    rest_swap, rest_mid = stage(rest_swap, rest_mid)
    rest_c = along_col(rest_mid, MID_END, every)
    rest_far = along_col(rest_swap, MID_MID, every)
    hop = along_col(mine, END_MID, every)
    corner_far, corner_c, mine = tied((corner_far, corner_c, mine))
    corner_cc = along_col(corner_far, MID_END, one)

    lead_c, lead_far, last_own, corner_c = tied((lead_c, lead_far, both(raw, rows), corner_c))
    lead_far, lead_c = stage(lead_far, lead_c)
    lead_cc = along_col(lead_far, MID_END, most)
    last_end = along_col(last_own, END_MID, every)
    corners = ordered(corner, corner_swap, corner_mid, corner_far, corner_c, corner_cc)
    corners, last_own = tied((corners, last_own))
    upper = along_row(corners[:half], ((1, 0),), ALL_COLS)
    corners = near(jnp.where(even, upper, corners[half:]))

    corners, rest_c, rest_far, hop = tied((corners, rest_c, rest_far, hop))
    rest_far, rest_c = stage(rest_far, rest_c)
    rest_cc = along_col(rest_far, MID_END, every)
    last_both = along_col(jnp.concatenate([last_own, last_end], axis=1), MID_MID, every)
    hop_other = along_row(hop, SWAP, ALL_COLS)
    corners = far(corners)
    held = jnp.concatenate([mine, corners], axis=0)
    other = along_row(held, SWAP, ALL_COLS)
    place = jnp.stack([even, left, end, row == 0, row == 1]).astype(jnp.int32)
    solved, corner_high, corner_low = solve_own(place, held, other, inverses)
    sent = solve_and_multiply(
        place, hop, hop_other, inverses, (corner_high, corner_low), (last_own, last_end, last_both)
    )
    returned = along_col(sent, MID_END, every)
    sent, lead_cc, rest_cc = tied((sent, lead_cc, rest_cc))
    groups = [
        (lead_own, lead_swap, lead_mid, lead_far, lead_c, lead_cc),
        (rest_own, rest_swap, rest_mid, rest_far, rest_c, rest_cc),
    ]
    out = update(place, test_kernel, solved, groups, (last_own, last_end, last_both))
    return finish(place, test_kernel, returned, out)


def solution(mesh):
    in_specs = (P("row", "col"), P("row", "col"), P("row", "col"), P(), P())
    out_specs = P("row", "col")
    body = four if dict(mesh.shape) == {"row": ROWS, "col": COLS} else general
    return jax.shard_map(body, mesh=mesh, in_specs=in_specs, out_specs=out_specs, check_vma=False)
```

```python
import functools

import jax
import jax.numpy as jnp
from jax import lax
from jax.experimental import pallas as pl
from jax.experimental.pallas import tpu as pltpu
from jax.sharding import PartitionSpec as P

STAGE_FLOPS = 4 * 10**10
FILLERS = 3


def product(left, right):
    return jnp.dot(left, right, precision=lax.Precision.HIGH, preferred_element_type=jnp.float32)


def broadcast(value, axis, source):
    kept = jnp.where(lax.axis_index(axis) == source, value, 0).astype(value.dtype)
    return lax.psum(kept, axis)


def general(test_kernel, first_panel, second_panel, first_inverse, second_inverse):
    block = first_inverse.shape[0]
    position = lax.axis_index("row")
    first_rows = broadcast(test_kernel[:block], "row", 0)
    first_solved = product(first_inverse, first_rows)
    partial_value = test_kernel - product(lax.all_gather(first_panel, "col", axis=1, tiled=True), first_solved)
    second_rows = broadcast(partial_value[:block], "row", 1)
    second_solved = product(second_inverse, second_rows)
    final = partial_value - product(lax.all_gather(second_panel, "col", axis=1, tiled=True), second_solved)
    leading_final = jnp.where(
        position == 0, first_solved, jnp.where(position == 1, second_solved, final[:block])
    )
    return final.at[:block].set(leading_final)


AXES = ("row", "col")
ROWS, COLS = 8, 4
END_MID = ((0, 1), (3, 2))
MID_MID = ((1, 2), (2, 1))
MID_END = ((1, 0), (2, 3))


def pairs_of(pairs, rows):
    return [(r * COLS + a, r * COLS + b) for r in rows for a, b in pairs]


def along_col(value, pairs, rows):
    return lax.ppermute(value, AXES, pairs_of(pairs, rows))


def along_row(value, pairs, cols):
    return lax.ppermute(value, AXES, [(a * COLS + c, b * COLS + c) for a, b in pairs for c in cols])


ALL_COLS = (0, 1, 2, 3)
SWAP = tuple((r, r ^ 1) for r in range(ROWS))


def split(value):
    high = value.astype(jnp.bfloat16)
    return high, (value - high.astype(jnp.float32)).astype(jnp.bfloat16)


def three_pass(left, right):
    def one(a, b):
        return jnp.dot(a, b, preferred_element_type=jnp.float32)

    return one(left[0], right[0]) + (one(left[0], right[1]) + one(left[1], right[0]))


TILE = 256
VMEM_BYTES = 56 * 2**20
SMEM = pl.BlockSpec(memory_space=pltpu.SMEM)


def halves(place, held, other):
    a, b = held[...], other[...]
    return jnp.where(place[0] == 1, a, b), jnp.where(place[0] == 1, b, a)


def solved_tile(place, tops, corners, inverses):
    low, high = halves(place, *tops)
    half = low.shape[0] // 2
    first_top = jnp.concatenate([low[:half], high[:half]], axis=0)
    second_top = jnp.concatenate([low[half:], high[half:]], axis=0)
    corner = jnp.concatenate(halves(place, *corners), axis=0)
    slab = first_top.shape[0] // COLS

    def turned(solved):
        pieces = [solved[k * slab : (k + 1) * slab] for k in range(COLS)]
        return [jnp.where(place[1] == 1, pieces[k], pieces[COLS - 1 - k]) for k in range(COLS)]

    first_high, first_low, second_high, second_low = (ref[...] for ref in inverses)
    first = turned(three_pass((first_high, first_low), split(first_top)))
    value = second_top - three_pass(split(corner), split(jnp.concatenate(first, axis=0)))
    second = turned(three_pass((second_high, second_low), split(value)))
    return jnp.concatenate([p for pair in zip(first, second) for p in pair], axis=0)


def split_kernel(one, two, *outs):
    outs[0][...], outs[1][...] = split(one[...])
    outs[2][...], outs[3][...] = split(two[...])


def split_inverses(one, two):
    return pl.pallas_call(
        split_kernel, out_shape=[jax.ShapeDtypeStruct(one.shape, jnp.bfloat16)] * 4
    )(one, two)


def solve_kernel(place, *refs):
    refs[8][...], refs[9][...] = split(solved_tile(place, refs[:2], refs[2:4], refs[4:8]))


def solve(place, tops, corners, inverses):
    rows, width = 2 * inverses[0].shape[0], tops[0].shape[1]
    part = jax.ShapeDtypeStruct((rows, width), jnp.bfloat16)
    return pl.pallas_call(
        solve_kernel,
        out_shape=[part, part],
        in_specs=[SMEM] + [pl.BlockSpec(memory_space=pltpu.VMEM)] * 8,
        compiler_params=pltpu.CompilerParams(vmem_limit_bytes=VMEM_BYTES),
        cost_estimate=pl.CostEstimate(flops=3 * 10**9, bytes_accessed=0, transcendentals=0),
    )(place, *tops, *corners, *inverses)


def multiply_kernel(near_end, own, both, high, low, out):
    panels = jnp.concatenate([near_end[...], own[...], both[...]], axis=1)
    out[...] = three_pass(split(panels), (high[...], low[...]))


def multiply(panels, solved):
    rows, width = panels[0].shape[0], solved[0].shape[1]
    return pl.pallas_call(
        multiply_kernel,
        grid=(rows // TILE,),
        out_shape=jax.ShapeDtypeStruct((rows, width), jnp.float32),
        in_specs=[pl.BlockSpec((TILE, v.shape[1]), lambda i: (i, 0)) for v in panels]
        + [pl.BlockSpec(v.shape, lambda i: (0, 0)) for v in solved],
        out_specs=pl.BlockSpec((TILE, width), lambda i: (i, 0)),
        compiler_params=pltpu.CompilerParams(vmem_limit_bytes=VMEM_BYTES),
        cost_estimate=pl.CostEstimate(flops=2 * 10**9, bytes_accessed=0, transcendentals=0),
    )(*panels, *solved)


def update_raw_kernel(blocks, place, top, high, low, own, swap, mid, far, c, cc, *outs):
    left, end, out = place[1] == 1, place[2] == 1, outs[-1]
    pairs = ((own, swap), (swap, own), (c, mid), (cc, far))
    panels = jnp.concatenate([jnp.where(end, a[...], b[...]) for a, b in pairs], axis=1)
    out[...] = top[...] - three_pass(split(panels), (high[...], low[...]))
    if blocks:
        slab = high.shape[0] // (2 * COLS)
        for which in range(2):
            @pl.when(place[3 + which] == 1)
            def _():
                for k in range(TILE // slab):
                    here = pl.program_id(0) * (TILE // slab) + k
                    here = jnp.where(left, here, COLS - 1 - here)
                    rows = pl.ds(pl.multiple_of((2 * here + which) * slab, slab), slab)
                    value = high[rows].astype(jnp.float32) + low[rows].astype(jnp.float32)
                    out[k * slab : (k + 1) * slab] = value


def update_raw(place, top, solved, group, first, blocks, *out):
    tile = pl.BlockSpec((TILE, top.shape[1]), lambda i: (first // TILE + i, 0))
    part = pl.BlockSpec((TILE, group[0].shape[1]), lambda i: (i, 0))
    return pl.pallas_call(
        functools.partial(update_raw_kernel, blocks),
        grid=(group[0].shape[0] // TILE,),
        out_shape=jax.ShapeDtypeStruct(top.shape, top.dtype),
        in_specs=[SMEM, tile]
        + [pl.BlockSpec(v.shape, lambda i: (0, 0)) for v in solved]
        + [part] * 6
        + [pl.BlockSpec(memory_space=pl.ANY)] * len(out),
        out_specs=tile,
        input_output_aliases={10: 0} if out else {},
        compiler_params=pltpu.CompilerParams(vmem_limit_bytes=VMEM_BYTES),
        cost_estimate=pl.CostEstimate(flops=3 * 10**9, bytes_accessed=0, transcendentals=0),
    )(place, top, *solved, *group, *out)


def finish_kernel(place, top, returned, near_end, own, both, high, low, kept, out):
    @pl.when(place[2] == 1)
    def _():
        out[...] = top[...] - returned[...]

    @pl.when(place[2] == 0)
    def _():
        panels = jnp.concatenate([near_end[...], own[...], both[...]], axis=1)
        out[...] = top[...] - three_pass(split(panels), (high[...], low[...]))


def finish(place, top, returned, last, solved, out):
    width, count = top.shape[1], returned.shape[0] // TILE
    first = top.shape[0] // TILE - count
    tile = pl.BlockSpec((TILE, width), lambda i: (first + i, 0))
    parts = (returned, *last)
    return pl.pallas_call(
        finish_kernel,
        grid=(count,),
        out_shape=jax.ShapeDtypeStruct(top.shape, top.dtype),
        in_specs=[SMEM, tile]
        + [pl.BlockSpec((TILE, v.shape[1]), lambda i: (i, 0)) for v in parts]
        + [pl.BlockSpec(v.shape, lambda i: (0, 0)) for v in solved]
        + [pl.BlockSpec(memory_space=pl.ANY)],
        out_specs=tile,
        input_output_aliases={8: 0},
        compiler_params=pltpu.CompilerParams(vmem_limit_bytes=VMEM_BYTES),
        cost_estimate=pl.CostEstimate(flops=2 * 10**9, bytes_accessed=0, transcendentals=0),
    )(place, top, *parts, *solved, out)


def nothing(*refs):
    pass


def hand_on(*values):
    anywhere = [pl.BlockSpec(memory_space=pl.ANY)] * len(values)
    return pl.pallas_call(
        nothing,
        out_shape=[jax.ShapeDtypeStruct(v.shape, v.dtype) for v in values],
        in_specs=anywhere,
        out_specs=anywhere,
        input_output_aliases={i: i for i in range(len(values))},
        compiler_params=pltpu.CompilerParams(vmem_limit_bytes=VMEM_BYTES),
        cost_estimate=pl.CostEstimate(flops=STAGE_FLOPS, bytes_accessed=0, transcendentals=0),
    )(*values)


def stage(token, *values):
    for _ in range(FILLERS):
        [token] = hand_on(token)
    return hand_on(token, *values)


def four(test_kernel, first_panel, second_panel, first_inverse, second_inverse):
    block = first_inverse.shape[0]
    rows, width = test_kernel.shape
    raw, slab = 3 * block, first_panel.shape[1]
    half = block // 2
    row, col = lax.axis_index("row"), lax.axis_index("col")
    end = (col == 0) | (col == COLS - 1)
    left = col < COLS // 2
    even = row % 2 == 0
    every, most = range(ROWS), range(1, ROWS)
    both_ways = END_MID + MID_END
    tied = lax.optimization_barrier

    def both(low, high):
        return jnp.concatenate([first_panel[low:high], second_panel[low:high]], axis=1)

    def near(mine):
        return along_row(mine, ((0, 2), (1, 5)), ALL_COLS)

    def far(mine):
        return along_row(mine, ((2, 6), (5, 7), (0, 4), (1, 3)), ALL_COLS)

    def near_or(got, mine):
        return jnp.where((row == 2) | (row == 5), got, mine)

    def far_or(got, mine):
        return jnp.where((row == 3) | (row == 4) | (row >= 6), got, mine)

    def ordered(own, swap, mid, far, c, cc):
        pairs = ((own, swap), (swap, own), (c, mid), (cc, far))
        return jnp.concatenate([jnp.where(end, a, b) for a, b in pairs], axis=1)

    place = jnp.stack([even, left, end, row == 0, row == 1]).astype(jnp.int32)

    lead_own, rest_own, last_own = both(0, block), both(block, raw), both(raw, rows)
    top = test_kernel[:block]
    given = along_row(jnp.where(even, top[half:], top[:half]), ((0, 1), (1, 0)), ALL_COLS)
    token = jnp.zeros((8, 128), jnp.float32)
    given, lead_own, rest_own = tied((given, lead_own, rest_own))

    mine = jnp.where(
        even,
        jnp.concatenate([top[:half], given], axis=0),
        jnp.concatenate([given, top[half:]], axis=0),
    )
    got = near(mine)
    lead_swap = along_col(lead_own, both_ways, most)
    lead_mid = along_col(lead_own, MID_MID, most)
    rest_swap = along_col(rest_own, both_ways, every)
    rest_mid = along_col(rest_own, MID_MID, every)
    token, lead_swap, lead_mid, got, last_own = stage(token, lead_swap, lead_mid, got, last_own)

    mine = near_or(got, mine)
    got = far(mine)
    crossed = lax.ppermute(
        jnp.where(end, last_own, lead_mid), AXES, pairs_of(MID_END, most) + pairs_of(END_MID, every)
    )
    lead_far = along_col(lead_swap, MID_MID, most)
    token, rest_swap, rest_mid, got = stage(token, rest_swap, rest_mid, got)

    mine = far_or(got, mine)
    token, crossed, lead_far = stage(token, crossed, lead_far)

    lead_cc = along_col(lead_far, MID_END, most)
    hop = along_col(mine, END_MID, every)
    rest_c = along_col(rest_mid, MID_END, every)
    rest_far = along_col(rest_swap, MID_MID, every)
    inverses = split_inverses(*tied((first_inverse, second_inverse, token))[:2])
    token, lead_cc = stage(token, lead_cc)

    slabs = [v[:, :slab] for v in (lead_own, lead_swap, lead_mid, lead_far, crossed, lead_cc)]
    corner = ordered(*slabs)
    upper = along_row(corner[:half], ((1, 0),), ALL_COLS)
    corner = jnp.where(even, upper, corner[half:])
    got = near(corner)
    last_sent = jnp.concatenate(tied((last_own, crossed, token))[:2], axis=1)
    last_both = along_col(last_sent, MID_MID, every)
    token, rest_far, hop, got = stage(token, rest_far, hop, got)

    corner = near_or(got, corner)
    got = far(corner)
    rest_cc = along_col(rest_far, MID_END, every)
    hop_other = along_row(hop, SWAP, ALL_COLS)
    token, rest_c, got, hop_other = stage(token, rest_c, got, hop_other)

    corner = far_or(got, corner)
    corner = (corner, along_row(corner, SWAP, ALL_COLS))
    mine, token = tied((mine, token))
    other = along_row(mine, SWAP, ALL_COLS)
    solved_end = solve(place, (hop, hop_other), corner, inverses)
    token, last_both, *solved_end = stage(token, last_both, *solved_end)

    last = (crossed, last_own, last_both)
    sent = multiply(last, solved_end)
    returned = along_col(sent, MID_END, every)
    sent, mine, other = tied((sent, mine, other))

    solved = solve(place, (mine, other), corner, inverses)
    lead = (lead_own, lead_swap, lead_mid, lead_far, crossed, lead_cc)
    out = update_raw(place, test_kernel, solved, lead, 0, True)
    token, rest_cc, out = stage(token, rest_cc, out)

    rest = (rest_own, rest_swap, rest_mid, rest_far, rest_c, rest_cc)
    out = update_raw(place, test_kernel, solved, rest, block, False, out)
    return finish(place, test_kernel, returned, last, solved, out)


def solution(mesh):
    in_specs = (P("row", "col"), P("row", "col"), P("row", "col"), P(), P())
    out_specs = P("row", "col")
    body = four if dict(mesh.shape) == {"row": ROWS, "col": COLS} else general
    return jax.shard_map(body, mesh=mesh, in_specs=in_specs, out_specs=out_specs, check_vma=False)
```

```python
import functools

import jax
import jax.numpy as jnp
from jax import lax
from jax.experimental import pallas as pl
from jax.experimental.pallas import tpu as pltpu
from jax.sharding import PartitionSpec as P

STAGE_FLOPS = 4 * 10**10
FILLERS = 2
STAGE_BYTES = 2**20


def product(left, right):
    return jnp.dot(left, right, precision=lax.Precision.HIGH, preferred_element_type=jnp.float32)


def broadcast(value, axis, source):
    kept = jnp.where(lax.axis_index(axis) == source, value, 0).astype(value.dtype)
    return lax.psum(kept, axis)


def general(test_kernel, first_panel, second_panel, first_inverse, second_inverse):
    block = first_inverse.shape[0]
    position = lax.axis_index("row")
    first_rows = broadcast(test_kernel[:block], "row", 0)
    first_solved = product(first_inverse, first_rows)
    partial_value = test_kernel - product(lax.all_gather(first_panel, "col", axis=1, tiled=True), first_solved)
    second_rows = broadcast(partial_value[:block], "row", 1)
    second_solved = product(second_inverse, second_rows)
    final = partial_value - product(lax.all_gather(second_panel, "col", axis=1, tiled=True), second_solved)
    leading_final = jnp.where(
        position == 0, first_solved, jnp.where(position == 1, second_solved, final[:block])
    )
    return final.at[:block].set(leading_final)


AXES = ("row", "col")
ROWS, COLS = 8, 4
END_MID = ((0, 1), (3, 2))
MID_MID = ((1, 2), (2, 1))
MID_END = ((1, 0), (2, 3))


def pairs_of(pairs, rows):
    return [(r * COLS + a, r * COLS + b) for r in rows for a, b in pairs]


def along_col(value, pairs, rows):
    return lax.ppermute(value, AXES, pairs_of(pairs, rows))


def along_row(value, pairs, cols):
    return lax.ppermute(value, AXES, [(a * COLS + c, b * COLS + c) for a, b in pairs for c in cols])


ALL_COLS = (0, 1, 2, 3)
SWAP = tuple((r, r ^ 1) for r in range(ROWS))


def split(value):
    high = value.astype(jnp.bfloat16)
    return high, (value - high.astype(jnp.float32)).astype(jnp.bfloat16)


def three_pass(left, right):
    def one(a, b):
        return jnp.dot(a, b, preferred_element_type=jnp.float32)

    return one(left[0], right[0]) + (one(left[0], right[1]) + one(left[1], right[0]))


TILE = 256
VMEM_BYTES = 32 * 2**20
SMEM = pl.BlockSpec(memory_space=pltpu.SMEM)


def halves(place, held, other):
    a, b = held[...], other[...]
    return jnp.where(place[0] == 1, a, b), jnp.where(place[0] == 1, b, a)


def solved_tile(place, tops, corners, inverses):
    low, high = halves(place, *tops)
    half = low.shape[0] // 2
    first_top = jnp.concatenate([low[:half], high[:half]], axis=0)
    second_top = jnp.concatenate([low[half:], high[half:]], axis=0)
    corner = jnp.concatenate(halves(place, *corners), axis=0)
    slab = first_top.shape[0] // COLS

    def turned(solved):
        pieces = [solved[k * slab : (k + 1) * slab] for k in range(COLS)]
        return [jnp.where(place[1] == 1, pieces[k], pieces[COLS - 1 - k]) for k in range(COLS)]

    first_high, first_low, second_high, second_low = (ref[...] for ref in inverses)
    first = turned(three_pass((first_high, first_low), split(first_top)))
    value = second_top - three_pass(split(corner), split(jnp.concatenate(first, axis=0)))
    second = turned(three_pass((second_high, second_low), split(value)))
    return jnp.concatenate([p for pair in zip(first, second) for p in pair], axis=0)


def split_kernel(one, two, *outs):
    outs[0][...], outs[1][...] = split(one[...])
    outs[2][...], outs[3][...] = split(two[...])


def split_inverses(one, two):
    return pl.pallas_call(
        split_kernel,
        out_shape=[jax.ShapeDtypeStruct(one.shape, jnp.bfloat16)] * 4,
        compiler_params=pltpu.CompilerParams(vmem_limit_bytes=16 * 2**20),
    )(one, two)


def solve_kernel(place, *refs):
    refs[8][...], refs[9][...] = split(solved_tile(place, refs[:2], refs[2:4], refs[4:8]))


def solve(place, tops, corners, inverses):
    rows, width = 2 * inverses[0].shape[0], tops[0].shape[1]
    part = jax.ShapeDtypeStruct((rows, width), jnp.bfloat16)
    return pl.pallas_call(
        solve_kernel,
        out_shape=[part, part],
        in_specs=[SMEM] + [pl.BlockSpec(memory_space=pltpu.VMEM)] * 8,
        compiler_params=pltpu.CompilerParams(vmem_limit_bytes=VMEM_BYTES),
        cost_estimate=pl.CostEstimate(flops=3 * 10**9, bytes_accessed=0, transcendentals=0),
    )(place, *tops, *corners, *inverses)


def multiply_kernel(near_end, own, both, high, low, out):
    panels = jnp.concatenate([near_end[...], own[...], both[...]], axis=1)
    out[...] = three_pass(split(panels), (high[...], low[...]))


def multiply(panels, solved):
    rows, width = panels[0].shape[0], solved[0].shape[1]
    return pl.pallas_call(
        multiply_kernel,
        grid=(rows // TILE,),
        out_shape=jax.ShapeDtypeStruct((rows, width), jnp.float32),
        in_specs=[pl.BlockSpec((TILE, v.shape[1]), lambda i: (i, 0)) for v in panels]
        + [pl.BlockSpec(v.shape, lambda i: (0, 0)) for v in solved],
        out_specs=pl.BlockSpec((TILE, width), lambda i: (i, 0)),
        compiler_params=pltpu.CompilerParams(vmem_limit_bytes=VMEM_BYTES),
        cost_estimate=pl.CostEstimate(flops=2 * 10**9, bytes_accessed=0, transcendentals=0),
    )(*panels, *solved)


def update_raw_kernel(blocks, place, top, high, low, own, swap, mid, far, c, cc, *outs):
    left, end, out = place[1] == 1, place[2] == 1, outs[-1]
    pairs = ((own, swap), (swap, own), (c, mid), (cc, far))
    panels = jnp.concatenate([jnp.where(end, a[...], b[...]) for a, b in pairs], axis=1)
    out[...] = top[...] - three_pass(split(panels), (high[...], low[...]))
    if blocks:
        slab = high.shape[0] // (2 * COLS)
        for which in range(2):
            @pl.when(place[3 + which] == 1)
            def _():
                for k in range(TILE // slab):
                    here = pl.program_id(0) * (TILE // slab) + k
                    here = jnp.where(left, here, COLS - 1 - here)
                    rows = pl.ds(pl.multiple_of((2 * here + which) * slab, slab), slab)
                    value = high[rows].astype(jnp.float32) + low[rows].astype(jnp.float32)
                    out[k * slab : (k + 1) * slab] = value


def update_raw(place, top, solved, group, first, blocks, *out):
    tile = pl.BlockSpec((TILE, top.shape[1]), lambda i: (first // TILE + i, 0))
    part = pl.BlockSpec((TILE, group[0].shape[1]), lambda i: (i, 0))
    return pl.pallas_call(
        functools.partial(update_raw_kernel, blocks),
        grid=(group[0].shape[0] // TILE,),
        out_shape=jax.ShapeDtypeStruct(top.shape, top.dtype),
        in_specs=[SMEM, tile]
        + [pl.BlockSpec(v.shape, lambda i: (0, 0)) for v in solved]
        + [part] * 6
        + [pl.BlockSpec(memory_space=pl.ANY)] * len(out),
        out_specs=tile,
        input_output_aliases={10: 0} if out else {},
        compiler_params=pltpu.CompilerParams(vmem_limit_bytes=VMEM_BYTES),
        cost_estimate=pl.CostEstimate(flops=3 * 10**9, bytes_accessed=0, transcendentals=0),
    )(place, top, *solved, *group, *out)


def update_last_kernel(place, top, near_end, own, both, high, low, kept, out):
    @pl.when(place[2] == 0)
    def _():
        panels = jnp.concatenate([near_end[...], own[...], both[...]], axis=1)
        out[...] = top[...] - three_pass(split(panels), (high[...], low[...]))


def finish_kernel(place, top, returned, kept, out):
    out[...] = jnp.where(place[2] == 1, top[...] - returned[...], kept[...])


def last_call(body, place, top, parts, fixed, out, block_of_out, flops):
    width, count = top.shape[1], parts[0].shape[0] // TILE
    first = top.shape[0] // TILE - count
    tile = pl.BlockSpec((TILE, width), lambda i: (first + i, 0))
    return pl.pallas_call(
        body,
        grid=(count,),
        out_shape=jax.ShapeDtypeStruct(top.shape, top.dtype),
        in_specs=[SMEM, tile]
        + [pl.BlockSpec((TILE, v.shape[1]), lambda i: (i, 0)) for v in parts]
        + [pl.BlockSpec(v.shape, lambda i: (0, 0)) for v in fixed]
        + [tile if block_of_out else pl.BlockSpec(memory_space=pl.ANY)],
        out_specs=tile,
        input_output_aliases={2 + len(parts) + len(fixed): 0},
        compiler_params=pltpu.CompilerParams(vmem_limit_bytes=VMEM_BYTES),
        cost_estimate=pl.CostEstimate(flops=flops, bytes_accessed=0, transcendentals=0),
    )(place, top, *parts, *fixed, out)


def update_last(place, top, last, solved, out):
    return last_call(update_last_kernel, place, top, last, solved, out, False, 2 * 10**9)


def finish(place, top, returned, out):
    return last_call(finish_kernel, place, top, (returned,), (), out, True, 10**9)


def nothing(*refs):
    pass


def hand_on(*values):
    anywhere = [pl.BlockSpec(memory_space=pl.ANY)] * len(values)
    return pl.pallas_call(
        nothing,
        out_shape=[jax.ShapeDtypeStruct(v.shape, v.dtype) for v in values],
        in_specs=anywhere,
        out_specs=anywhere,
        input_output_aliases={i: i for i in range(len(values))},
        compiler_params=pltpu.CompilerParams(vmem_limit_bytes=STAGE_BYTES),
        cost_estimate=pl.CostEstimate(flops=STAGE_FLOPS, bytes_accessed=0, transcendentals=0),
    )(*values)


def stage(token, *values):
    for _ in range(FILLERS):
        [token] = hand_on(token)
    return hand_on(token, *values)


def four(test_kernel, first_panel, second_panel, first_inverse, second_inverse):
    block = first_inverse.shape[0]
    rows, width = test_kernel.shape
    raw, slab = 3 * block, first_panel.shape[1]
    half = block // 2
    row, col = lax.axis_index("row"), lax.axis_index("col")
    end = (col == 0) | (col == COLS - 1)
    left = col < COLS // 2
    even = row % 2 == 0
    every, most = range(ROWS), range(1, ROWS)
    both_ways = END_MID + MID_END
    tied = lax.optimization_barrier

    def both(low, high):
        return jnp.concatenate([first_panel[low:high], second_panel[low:high]], axis=1)

    def near(mine):
        return along_row(mine, ((0, 2), (1, 5)), ALL_COLS)

    def far(mine):
        return along_row(mine, ((2, 6), (5, 7), (0, 4), (1, 3)), ALL_COLS)

    def near_or(got, mine):
        return jnp.where((row == 2) | (row == 5), got, mine)

    def far_or(got, mine):
        return jnp.where((row == 3) | (row == 4) | (row >= 6), got, mine)

    def ordered(own, swap, mid, far, c, cc):
        pairs = ((own, swap), (swap, own), (c, mid), (cc, far))
        return jnp.concatenate([jnp.where(end, a, b) for a, b in pairs], axis=1)

    place = jnp.stack([even, left, end, row == 0, row == 1]).astype(jnp.int32)

    lead_own, rest_own, last_own = both(0, block), both(block, raw), both(raw, rows)
    top = test_kernel[:block]
    given, lead_own = tied((jnp.where(even, top[half:], top[:half]), lead_own))
    given = along_row(given, ((0, 1), (1, 0)), ALL_COLS)
    token = jnp.zeros((8, 128), jnp.float32)
    given, rest_own = tied((given, rest_own))

    mine = jnp.where(
        even,
        jnp.concatenate([top[:half], given], axis=0),
        jnp.concatenate([given, top[half:]], axis=0),
    )
    got = near(mine)
    lead_swap = along_col(lead_own, both_ways, most)
    lead_mid = along_col(lead_own, MID_MID, most)
    rest_swap = along_col(rest_own, both_ways, every)
    rest_mid = along_col(rest_own, MID_MID, every)
    token, lead_swap, lead_mid, got, last_own = stage(token, lead_swap, lead_mid, got, last_own)

    mine = near_or(got, mine)
    got = far(mine)
    crossed = lax.ppermute(
        jnp.where(end, last_own, lead_mid), AXES, pairs_of(MID_END, most) + pairs_of(END_MID, every)
    )
    lead_far = along_col(lead_swap, MID_MID, most)
    token, rest_swap, rest_mid, got = stage(token, rest_swap, rest_mid, got)

    mine = far_or(got, mine)
    hop = along_col(mine, END_MID, every)
    rest_far = along_col(rest_swap, MID_MID, every)
    inverses = split_inverses(*tied((first_inverse, second_inverse, token))[:2])
    token, crossed, lead_far = stage(token, crossed, lead_far)

    lead_cc = along_col(lead_far, MID_END, most)
    rest_c = along_col(rest_mid, MID_END, every)
    token, lead_cc = stage(token, lead_cc)

    slabs = [v[:, :slab] for v in (lead_own, lead_swap, lead_mid, lead_far, crossed, lead_cc)]
    corner = ordered(*slabs)
    upper = along_row(corner[:half], ((1, 0),), ALL_COLS)
    corner = jnp.where(even, upper, corner[half:])
    got = near(corner)
    last_sent = jnp.concatenate(tied((last_own, crossed, token))[:2], axis=1)
    last_both = along_col(last_sent, MID_MID, every)
    token, rest_far, hop, got = stage(token, rest_far, hop, got)

    corner = near_or(got, corner)
    got = far(corner)
    rest_cc = along_col(rest_far, MID_END, every)
    hop_other = along_row(hop, SWAP, ALL_COLS)
    token, rest_c, got, hop_other = stage(token, rest_c, got, hop_other)

    corner = far_or(got, corner)
    corner = (corner, along_row(corner, SWAP, ALL_COLS))
    mine, token = tied((mine, token))
    other = along_row(mine, SWAP, ALL_COLS)
    solved_end = solve(place, (hop, hop_other), corner, inverses)
    token, last_both, *solved_end = stage(token, last_both, *solved_end)

    last = (crossed, last_own, last_both)
    sent = multiply(last, solved_end)
    returned = along_col(sent, MID_END, every)
    sent, mine, other = tied((sent, mine, other))

    solved = solve(place, (mine, other), corner, inverses)
    lead = (lead_own, lead_swap, lead_mid, lead_far, crossed, lead_cc)
    out = update_raw(place, test_kernel, solved, lead, 0, True)
    token, rest_cc, out = stage(token, rest_cc, out)

    rest = (rest_own, rest_swap, rest_mid, rest_far, rest_c, rest_cc)
    out = update_raw(place, test_kernel, solved, rest, block, False, out)
    out = update_last(place, test_kernel, last, solved, out)
    return finish(place, test_kernel, returned, out)


def solution(mesh):
    in_specs = (P("row", "col"), P("row", "col"), P("row", "col"), P(), P())
    out_specs = P("row", "col")
    body = four if dict(mesh.shape) == {"row": ROWS, "col": COLS} else general
    return jax.shard_map(body, mesh=mesh, in_specs=in_specs, out_specs=out_specs, check_vma=False)
```

```python
import functools

import jax
import jax.numpy as jnp
from jax import lax
from jax.experimental import pallas as pl
from jax.experimental.pallas import tpu as pltpu
from jax.sharding import PartitionSpec as P

STAGE_FLOPS = 10**10
FILLERS = 2
STAGE_BYTES = 2**20


def product(left, right):
    return jnp.dot(left, right, precision=lax.Precision.HIGH, preferred_element_type=jnp.float32)


def broadcast(value, axis, source):
    kept = jnp.where(lax.axis_index(axis) == source, value, 0).astype(value.dtype)
    return lax.psum(kept, axis)


def general(test_kernel, first_panel, second_panel, first_inverse, second_inverse):
    block = first_inverse.shape[0]
    position = lax.axis_index("row")
    first_rows = broadcast(test_kernel[:block], "row", 0)
    first_solved = product(first_inverse, first_rows)
    partial_value = test_kernel - product(lax.all_gather(first_panel, "col", axis=1, tiled=True), first_solved)
    second_rows = broadcast(partial_value[:block], "row", 1)
    second_solved = product(second_inverse, second_rows)
    final = partial_value - product(lax.all_gather(second_panel, "col", axis=1, tiled=True), second_solved)
    leading_final = jnp.where(
        position == 0, first_solved, jnp.where(position == 1, second_solved, final[:block])
    )
    return final.at[:block].set(leading_final)


AXES = ("row", "col")
ROWS, COLS = 8, 4
END_MID = ((0, 1), (3, 2))
MID_MID = ((1, 2), (2, 1))
MID_END = ((1, 0), (2, 3))


def pairs_of(pairs, rows):
    return [(r * COLS + a, r * COLS + b) for r in rows for a, b in pairs]


def along_col(value, pairs, rows):
    return lax.ppermute(value, AXES, pairs_of(pairs, rows))


def along_row(value, pairs, cols):
    return lax.ppermute(value, AXES, [(a * COLS + c, b * COLS + c) for a, b in pairs for c in cols])


ALL_COLS = (0, 1, 2, 3)
SWAP = tuple((r, r ^ 1) for r in range(ROWS))


def split(value):
    high = value.astype(jnp.bfloat16)
    return high, (value - high.astype(jnp.float32)).astype(jnp.bfloat16)


def three_pass(left, right):
    def one(a, b):
        return jnp.dot(a, b, preferred_element_type=jnp.float32)

    return one(left[0], right[0]) + (one(left[0], right[1]) + one(left[1], right[0]))


TILE = 256
VMEM_BYTES = 32 * 2**20
SMEM = pl.BlockSpec(memory_space=pltpu.SMEM)


def halves(place, held, other):
    a, b = held[...], other[...]
    return jnp.where(place[0] == 1, a, b), jnp.where(place[0] == 1, b, a)


def solved_tile(place, tops, corners, inverses):
    low, high = halves(place, *tops)
    half = low.shape[0] // 2
    first_top = jnp.concatenate([low[:half], high[:half]], axis=0)
    second_top = jnp.concatenate([low[half:], high[half:]], axis=0)
    corner = jnp.concatenate(halves(place, *corners), axis=0)
    slab = first_top.shape[0] // COLS

    def turned(solved):
        pieces = [solved[k * slab : (k + 1) * slab] for k in range(COLS)]
        return [jnp.where(place[1] == 1, pieces[k], pieces[COLS - 1 - k]) for k in range(COLS)]

    first_high, first_low, second_high, second_low = (ref[...] for ref in inverses)
    first = turned(three_pass((first_high, first_low), split(first_top)))
    value = second_top - three_pass(split(corner), split(jnp.concatenate(first, axis=0)))
    second = turned(three_pass((second_high, second_low), split(value)))
    return jnp.concatenate([p for pair in zip(first, second) for p in pair], axis=0)


def split_kernel(one, two, *outs):
    outs[0][...], outs[1][...] = split(one[...])
    outs[2][...], outs[3][...] = split(two[...])


def split_inverses(one, two):
    return pl.pallas_call(
        split_kernel,
        out_shape=[jax.ShapeDtypeStruct(one.shape, jnp.bfloat16)] * 4,
        compiler_params=pltpu.CompilerParams(vmem_limit_bytes=16 * 2**20),
    )(one, two)


def solve_kernel(place, *refs):
    refs[8][...], refs[9][...] = split(solved_tile(place, refs[:2], refs[2:4], refs[4:8]))


def solve(place, tops, corners, inverses):
    rows, width = 2 * inverses[0].shape[0], tops[0].shape[1]
    part = jax.ShapeDtypeStruct((rows, width), jnp.bfloat16)
    return pl.pallas_call(
        solve_kernel,
        out_shape=[part, part],
        in_specs=[SMEM] + [pl.BlockSpec(memory_space=pltpu.VMEM)] * 8,
        compiler_params=pltpu.CompilerParams(vmem_limit_bytes=VMEM_BYTES),
        cost_estimate=pl.CostEstimate(flops=3 * 10**9, bytes_accessed=0, transcendentals=0),
    )(place, *tops, *corners, *inverses)


def multiply_kernel(near_end, own, both, high, low, out):
    panels = jnp.concatenate([near_end[...], own[...], both[...]], axis=1)
    out[...] = three_pass(split(panels), (high[...], low[...]))


def multiply(panels, solved):
    rows, width = panels[0].shape[0], solved[0].shape[1]
    return pl.pallas_call(
        multiply_kernel,
        grid=(rows // TILE,),
        out_shape=jax.ShapeDtypeStruct((rows, width), jnp.float32),
        in_specs=[pl.BlockSpec((TILE, v.shape[1]), lambda i: (i, 0)) for v in panels]
        + [pl.BlockSpec(v.shape, lambda i: (0, 0)) for v in solved],
        out_specs=pl.BlockSpec((TILE, width), lambda i: (i, 0)),
        compiler_params=pltpu.CompilerParams(vmem_limit_bytes=VMEM_BYTES),
        cost_estimate=pl.CostEstimate(flops=2 * 10**9, bytes_accessed=0, transcendentals=0),
    )(*panels, *solved)


def update_raw_kernel(blocks, place, top, high, low, own, swap, mid, far, c, cc, *outs):
    left, end, out = place[1] == 1, place[2] == 1, outs[-1]
    pairs = ((own, swap), (swap, own), (c, mid), (cc, far))
    panels = jnp.concatenate([jnp.where(end, a[...], b[...]) for a, b in pairs], axis=1)
    out[...] = top[...] - three_pass(split(panels), (high[...], low[...]))
    if blocks:
        slab = high.shape[0] // (2 * COLS)
        for which in range(2):
            @pl.when(place[3 + which] == 1)
            def _():
                for k in range(TILE // slab):
                    here = pl.program_id(0) * (TILE // slab) + k
                    here = jnp.where(left, here, COLS - 1 - here)
                    rows = pl.ds(pl.multiple_of((2 * here + which) * slab, slab), slab)
                    value = high[rows].astype(jnp.float32) + low[rows].astype(jnp.float32)
                    out[k * slab : (k + 1) * slab] = value


def update_raw(place, top, solved, group, first, blocks, *out):
    tile = pl.BlockSpec((TILE, top.shape[1]), lambda i: (first // TILE + i, 0))
    part = pl.BlockSpec((TILE, group[0].shape[1]), lambda i: (i, 0))
    return pl.pallas_call(
        functools.partial(update_raw_kernel, blocks),
        grid=(group[0].shape[0] // TILE,),
        out_shape=jax.ShapeDtypeStruct(top.shape, top.dtype),
        in_specs=[SMEM, tile]
        + [pl.BlockSpec(v.shape, lambda i: (0, 0)) for v in solved]
        + [part] * 6
        + [pl.BlockSpec(memory_space=pl.ANY)] * len(out),
        out_specs=tile,
        input_output_aliases={10: 0} if out else {},
        compiler_params=pltpu.CompilerParams(vmem_limit_bytes=VMEM_BYTES),
        cost_estimate=pl.CostEstimate(flops=3 * 10**9, bytes_accessed=0, transcendentals=0),
    )(place, top, *solved, *group, *out)


def update_last_kernel(place, top, near_end, own, both, high, low, kept, out):
    @pl.when(place[2] == 0)
    def _():
        panels = jnp.concatenate([near_end[...], own[...], both[...]], axis=1)
        out[...] = top[...] - three_pass(split(panels), (high[...], low[...]))


def finish_kernel(place, top, returned, kept, out):
    out[...] = jnp.where(place[2] == 1, top[...] - returned[...], kept[...])


def last_call(body, place, top, parts, fixed, out, block_of_out, flops):
    width, count = top.shape[1], parts[0].shape[0] // TILE
    first = top.shape[0] // TILE - count
    tile = pl.BlockSpec((TILE, width), lambda i: (first + i, 0))
    return pl.pallas_call(
        body,
        grid=(count,),
        out_shape=jax.ShapeDtypeStruct(top.shape, top.dtype),
        in_specs=[SMEM, tile]
        + [pl.BlockSpec((TILE, v.shape[1]), lambda i: (i, 0)) for v in parts]
        + [pl.BlockSpec(v.shape, lambda i: (0, 0)) for v in fixed]
        + [tile if block_of_out else pl.BlockSpec(memory_space=pl.ANY)],
        out_specs=tile,
        input_output_aliases={2 + len(parts) + len(fixed): 0},
        compiler_params=pltpu.CompilerParams(vmem_limit_bytes=VMEM_BYTES),
        cost_estimate=pl.CostEstimate(flops=flops, bytes_accessed=0, transcendentals=0),
    )(place, top, *parts, *fixed, out)


def update_last(place, top, last, solved, out):
    return last_call(update_last_kernel, place, top, last, solved, out, False, 2 * 10**9)


def finish(place, top, returned, out):
    return last_call(finish_kernel, place, top, (returned,), (), out, True, 10**9)


def nothing(*refs):
    pass


def hand_on(*values):
    anywhere = [pl.BlockSpec(memory_space=pl.ANY)] * len(values)
    return pl.pallas_call(
        nothing,
        out_shape=[jax.ShapeDtypeStruct(v.shape, v.dtype) for v in values],
        in_specs=anywhere,
        out_specs=anywhere,
        input_output_aliases={i: i for i in range(len(values))},
        compiler_params=pltpu.CompilerParams(vmem_limit_bytes=STAGE_BYTES),
        cost_estimate=pl.CostEstimate(flops=STAGE_FLOPS, bytes_accessed=0, transcendentals=0),
    )(*values)


def stage(token, *values):
    for _ in range(FILLERS):
        [token] = hand_on(token)
    return hand_on(token, *values)


def four(test_kernel, first_panel, second_panel, first_inverse, second_inverse):
    block = first_inverse.shape[0]
    rows, width = test_kernel.shape
    raw, slab = 3 * block, first_panel.shape[1]
    half = block // 2
    row, col = lax.axis_index("row"), lax.axis_index("col")
    end = (col == 0) | (col == COLS - 1)
    left = col < COLS // 2
    even = row % 2 == 0
    every, most = range(ROWS), range(1, ROWS)
    both_ways = END_MID + MID_END
    tied = lax.optimization_barrier

    def both(low, high):
        return jnp.concatenate([first_panel[low:high], second_panel[low:high]], axis=1)

    def near(mine):
        return along_row(mine, ((0, 2), (1, 5)), ALL_COLS)

    def far(mine):
        return along_row(mine, ((2, 6), (5, 7), (0, 4), (1, 3)), ALL_COLS)

    def near_or(got, mine):
        return jnp.where((row == 2) | (row == 5), got, mine)

    def far_or(got, mine):
        return jnp.where((row == 3) | (row == 4) | (row >= 6), got, mine)

    def ordered(own, swap, mid, far, c, cc):
        pairs = ((own, swap), (swap, own), (c, mid), (cc, far))
        return jnp.concatenate([jnp.where(end, a, b) for a, b in pairs], axis=1)

    place = jnp.stack([even, left, end, row == 0, row == 1]).astype(jnp.int32)

    lead_own, rest_own, last_own = both(0, block), both(block, raw), both(raw, rows)
    top = test_kernel[:block]
    top, lead_own = tied((top, lead_own))
    given = along_row(jnp.where(even, top[half:], top[:half]), ((0, 1), (1, 0)), ALL_COLS)
    token = jnp.zeros((8, 128), jnp.float32)
    given, rest_own = tied((given, rest_own))

    mine = jnp.where(
        even,
        jnp.concatenate([top[:half], given], axis=0),
        jnp.concatenate([given, top[half:]], axis=0),
    )
    got = near(mine)
    lead_swap = along_col(lead_own, both_ways, most)
    lead_mid = along_col(lead_own, MID_MID, most)
    rest_swap = along_col(rest_own, both_ways, every)
    rest_mid = along_col(rest_own, MID_MID, every)
    token, lead_swap, lead_mid, got, last_own = stage(token, lead_swap, lead_mid, got, last_own)

    mine = near_or(got, mine)
    got = far(mine)
    crossed = lax.ppermute(
        jnp.where(end, last_own, lead_mid), AXES, pairs_of(MID_END, most) + pairs_of(END_MID, every)
    )
    lead_far = along_col(lead_swap, MID_MID, most)
    token, rest_swap, rest_mid, got = stage(token, rest_swap, rest_mid, got)

    mine = far_or(got, mine)
    hop = along_col(mine, END_MID, every)
    rest_far = along_col(rest_swap, MID_MID, every)
    inverses = split_inverses(*tied((first_inverse, second_inverse, token))[:2])
    token, crossed, lead_far = stage(token, crossed, lead_far)

    lead_cc = along_col(lead_far, MID_END, most)
    rest_c = along_col(rest_mid, MID_END, every)
    token, lead_cc = stage(token, lead_cc)

    slabs = [v[:, :slab] for v in (lead_own, lead_swap, lead_mid, lead_far, crossed, lead_cc)]
    corner = ordered(*slabs)
    upper = along_row(corner[:half], ((1, 0),), ALL_COLS)
    corner = jnp.where(even, upper, corner[half:])
    got = near(corner)
    last_sent = jnp.concatenate(tied((last_own, crossed, token))[:2], axis=1)
    last_both = along_col(last_sent, MID_MID, every)
    token, rest_far, hop, got = stage(token, rest_far, hop, got)

    corner = near_or(got, corner)
    got = far(corner)
    rest_cc = along_col(rest_far, MID_END, every)
    hop_other = along_row(hop, SWAP, ALL_COLS)
    token, rest_c, got, hop_other = stage(token, rest_c, got, hop_other)

    corner = far_or(got, corner)
    corner = (corner, along_row(corner, SWAP, ALL_COLS))
    mine, token = tied((mine, token))
    other = along_row(mine, SWAP, ALL_COLS)
    solved_end = solve(place, (hop, hop_other), corner, inverses)
    token, last_both, *solved_end = stage(token, last_both, *solved_end)

    last = (crossed, last_own, last_both)
    sent = multiply(last, solved_end)
    returned = along_col(sent, MID_END, every)
    sent, mine, other = tied((sent, mine, other))

    solved = solve(place, (mine, other), corner, inverses)
    lead = (lead_own, lead_swap, lead_mid, lead_far, crossed, lead_cc)
    out = update_raw(place, test_kernel, solved, lead, 0, True)
    token, rest_cc, out = stage(token, rest_cc, out)

    rest = (rest_own, rest_swap, rest_mid, rest_far, rest_c, rest_cc)
    out = update_raw(place, test_kernel, solved, rest, block, False, out)
    out = update_last(place, test_kernel, last, solved, out)
    return finish(place, test_kernel, returned, out)


def solution(mesh):
    in_specs = (P("row", "col"), P("row", "col"), P("row", "col"), P(), P())
    out_specs = P("row", "col")
    body = four if dict(mesh.shape) == {"row": ROWS, "col": COLS} else general
    return jax.shard_map(body, mesh=mesh, in_specs=in_specs, out_specs=out_specs, check_vma=False)
```

```python
import functools

import jax
import jax.numpy as jnp
from jax import lax
from jax.experimental import pallas as pl
from jax.experimental.pallas import tpu as pltpu
from jax.sharding import PartitionSpec as P

STAGE_FLOPS = 10**10
FILLERS = 2
STAGE_BYTES = 2**20


def product(left, right):
    return jnp.dot(left, right, precision=lax.Precision.HIGH, preferred_element_type=jnp.float32)


def broadcast(value, axis, source):
    kept = jnp.where(lax.axis_index(axis) == source, value, 0).astype(value.dtype)
    return lax.psum(kept, axis)


def general(test_kernel, first_panel, second_panel, first_inverse, second_inverse):
    block = first_inverse.shape[0]
    position = lax.axis_index("row")
    first_rows = broadcast(test_kernel[:block], "row", 0)
    first_solved = product(first_inverse, first_rows)
    partial_value = test_kernel - product(lax.all_gather(first_panel, "col", axis=1, tiled=True), first_solved)
    second_rows = broadcast(partial_value[:block], "row", 1)
    second_solved = product(second_inverse, second_rows)
    final = partial_value - product(lax.all_gather(second_panel, "col", axis=1, tiled=True), second_solved)
    leading_final = jnp.where(
        position == 0, first_solved, jnp.where(position == 1, second_solved, final[:block])
    )
    return final.at[:block].set(leading_final)


AXES = ("row", "col")
ROWS, COLS = 8, 4
END_MID = ((0, 1), (3, 2))
MID_MID = ((1, 2), (2, 1))
MID_END = ((1, 0), (2, 3))


def pairs_of(pairs, rows):
    return [(r * COLS + a, r * COLS + b) for r in rows for a, b in pairs]


def along_col(value, pairs, rows):
    return lax.ppermute(value, AXES, pairs_of(pairs, rows))


def along_row(value, pairs, cols):
    return lax.ppermute(value, AXES, [(a * COLS + c, b * COLS + c) for a, b in pairs for c in cols])


ALL_COLS = (0, 1, 2, 3)
SWAP = tuple((r, r ^ 1) for r in range(ROWS))


def split(value):
    high = value.astype(jnp.bfloat16)
    return high, (value - high.astype(jnp.float32)).astype(jnp.bfloat16)


def three_pass(left, right):
    def one(a, b):
        return jnp.dot(a, b, preferred_element_type=jnp.float32)

    return one(left[0], right[0]) + (one(left[0], right[1]) + one(left[1], right[0]))


TILE = 256
VMEM_BYTES = 32 * 2**20
SMEM = pl.BlockSpec(memory_space=pltpu.SMEM)


def halves(place, held, other):
    a, b = held[...], other[...]
    return jnp.where(place[0] == 1, a, b), jnp.where(place[0] == 1, b, a)


def solved_tile(place, tops, corners, inverses):
    low, high = halves(place, *tops)
    half = low.shape[0] // 2
    first_top = jnp.concatenate([low[:half], high[:half]], axis=0)
    second_top = jnp.concatenate([low[half:], high[half:]], axis=0)
    corner = jnp.concatenate(halves(place, *corners), axis=0)
    slab = first_top.shape[0] // COLS

    def turned(solved):
        pieces = [solved[k * slab : (k + 1) * slab] for k in range(COLS)]
        return [jnp.where(place[1] == 1, pieces[k], pieces[COLS - 1 - k]) for k in range(COLS)]

    first_high, first_low, second_high, second_low = (ref[...] for ref in inverses)
    first = turned(three_pass((first_high, first_low), split(first_top)))
    value = second_top - three_pass(split(corner), split(jnp.concatenate(first, axis=0)))
    second = turned(three_pass((second_high, second_low), split(value)))
    return jnp.concatenate([p for pair in zip(first, second) for p in pair], axis=0)


def split_kernel(one, two, *outs):
    outs[0][...], outs[1][...] = split(one[...])
    outs[2][...], outs[3][...] = split(two[...])


def split_inverses(one, two):
    return pl.pallas_call(
        split_kernel,
        out_shape=[jax.ShapeDtypeStruct(one.shape, jnp.bfloat16)] * 4,
        compiler_params=pltpu.CompilerParams(vmem_limit_bytes=16 * 2**20),
    )(one, two)


def solve_kernel(place, *refs):
    refs[8][...], refs[9][...] = split(solved_tile(place, refs[:2], refs[2:4], refs[4:8]))


def solve(place, tops, corners, inverses):
    rows, width = 2 * inverses[0].shape[0], tops[0].shape[1]
    part = jax.ShapeDtypeStruct((rows, width), jnp.bfloat16)
    return pl.pallas_call(
        solve_kernel,
        out_shape=[part, part],
        in_specs=[SMEM] + [pl.BlockSpec(memory_space=pltpu.VMEM)] * 8,
        compiler_params=pltpu.CompilerParams(vmem_limit_bytes=VMEM_BYTES),
        cost_estimate=pl.CostEstimate(flops=3 * 10**9, bytes_accessed=0, transcendentals=0),
    )(place, *tops, *corners, *inverses)


def multiply_kernel(near_end, own, both, high, low, *outs):
    panels = jnp.concatenate([near_end[...], own[...], both[...]], axis=1)
    value = three_pass(split(panels), (high[...], low[...]))
    for i, out in enumerate(outs):
        out[...] = value[i * TILE : (i + 1) * TILE]


def multiply(panels, solved):
    rows, width = panels[0].shape[0], solved[0].shape[1]
    return pl.pallas_call(
        multiply_kernel,
        out_shape=[jax.ShapeDtypeStruct((TILE, width), jnp.float32)] * (rows // TILE),
        compiler_params=pltpu.CompilerParams(vmem_limit_bytes=VMEM_BYTES),
        cost_estimate=pl.CostEstimate(flops=2 * 10**9, bytes_accessed=0, transcendentals=0),
    )(*panels, *solved)


def update_raw_kernel(blocks, place, top, high, low, own, swap, mid, far, c, cc, *outs):
    left, end, out = place[1] == 1, place[2] == 1, outs[-1]
    pairs = ((own, swap), (swap, own), (c, mid), (cc, far))
    panels = jnp.concatenate([jnp.where(end, a[...], b[...]) for a, b in pairs], axis=1)
    out[...] = top[...] - three_pass(split(panels), (high[...], low[...]))
    if blocks:
        slab = high.shape[0] // (2 * COLS)
        for which in range(2):
            @pl.when(place[3 + which] == 1)
            def _():
                for k in range(TILE // slab):
                    here = pl.program_id(0) * (TILE // slab) + k
                    here = jnp.where(left, here, COLS - 1 - here)
                    rows = pl.ds(pl.multiple_of((2 * here + which) * slab, slab), slab)
                    value = high[rows].astype(jnp.float32) + low[rows].astype(jnp.float32)
                    out[k * slab : (k + 1) * slab] = value


def update_raw(place, top, solved, group, first, blocks, *out):
    tile = pl.BlockSpec((TILE, top.shape[1]), lambda i: (first // TILE + i, 0))
    part = pl.BlockSpec((TILE, group[0].shape[1]), lambda i: (i, 0))
    return pl.pallas_call(
        functools.partial(update_raw_kernel, blocks),
        grid=(group[0].shape[0] // TILE,),
        out_shape=jax.ShapeDtypeStruct(top.shape, top.dtype),
        in_specs=[SMEM, tile]
        + [pl.BlockSpec(v.shape, lambda i: (0, 0)) for v in solved]
        + [part] * 6
        + [pl.BlockSpec(memory_space=pl.ANY)] * len(out),
        out_specs=tile,
        input_output_aliases={10: 0} if out else {},
        compiler_params=pltpu.CompilerParams(vmem_limit_bytes=VMEM_BYTES),
        cost_estimate=pl.CostEstimate(flops=3 * 10**9, bytes_accessed=0, transcendentals=0),
    )(place, top, *solved, *group, *out)


def update_last_kernel(place, top, near_end, own, both, high, low, kept, out):
    @pl.when(place[2] == 0)
    def _():
        panels = jnp.concatenate([near_end[...], own[...], both[...]], axis=1)
        out[...] = top[...] - three_pass(split(panels), (high[...], low[...]))


def finish_kernel(place, top, returned, kept, out):
    out[...] = jnp.where(place[2] == 1, top[...] - returned[...], kept[...])


def last_call(body, place, top, parts, fixed, out, block_of_out, flops, past):
    width, count = top.shape[1], parts[0].shape[0] // TILE
    first = past // TILE - count
    tile = pl.BlockSpec((TILE, width), lambda i: (first + i, 0))
    return pl.pallas_call(
        body,
        grid=(count,),
        out_shape=jax.ShapeDtypeStruct(top.shape, top.dtype),
        in_specs=[SMEM, tile]
        + [pl.BlockSpec((TILE, v.shape[1]), lambda i: (i, 0)) for v in parts]
        + [pl.BlockSpec(v.shape, lambda i: (0, 0)) for v in fixed]
        + [tile if block_of_out else pl.BlockSpec(memory_space=pl.ANY)],
        out_specs=tile,
        input_output_aliases={2 + len(parts) + len(fixed): 0},
        compiler_params=pltpu.CompilerParams(vmem_limit_bytes=VMEM_BYTES),
        cost_estimate=pl.CostEstimate(flops=flops, bytes_accessed=0, transcendentals=0),
    )(place, top, *parts, *fixed, out)


def update_last(place, top, last, solved, out):
    return last_call(update_last_kernel, place, top, last, solved, out, False, 2 * 10**9, top.shape[0])


def finish(place, top, returned, out, past):
    return last_call(finish_kernel, place, top, (returned,), (), out, True, 10**9, past)


def nothing(*refs):
    pass


def hand_on(*values):
    anywhere = [pl.BlockSpec(memory_space=pl.ANY)] * len(values)
    return pl.pallas_call(
        nothing,
        out_shape=[jax.ShapeDtypeStruct(v.shape, v.dtype) for v in values],
        in_specs=anywhere,
        out_specs=anywhere,
        input_output_aliases={i: i for i in range(len(values))},
        compiler_params=pltpu.CompilerParams(vmem_limit_bytes=STAGE_BYTES),
        cost_estimate=pl.CostEstimate(flops=STAGE_FLOPS, bytes_accessed=0, transcendentals=0),
    )(*values)


def stage(token, *values):
    for _ in range(FILLERS):
        [token] = hand_on(token)
    return hand_on(token, *values)


def four(test_kernel, first_panel, second_panel, first_inverse, second_inverse):
    block = first_inverse.shape[0]
    rows, width = test_kernel.shape
    raw, slab = 3 * block, first_panel.shape[1]
    half = block // 2
    row, col = lax.axis_index("row"), lax.axis_index("col")
    end = (col == 0) | (col == COLS - 1)
    left = col < COLS // 2
    even = row % 2 == 0
    every, most = range(ROWS), range(1, ROWS)
    both_ways = END_MID + MID_END
    tied = lax.optimization_barrier

    def both(low, high):
        return jnp.concatenate([first_panel[low:high], second_panel[low:high]], axis=1)

    def near(mine):
        return along_row(mine, ((0, 2), (1, 5)), ALL_COLS)

    def far(mine):
        return along_row(mine, ((2, 6), (5, 7), (0, 4), (1, 3)), ALL_COLS)

    def near_or(got, mine):
        return jnp.where((row == 2) | (row == 5), got, mine)

    def far_or(got, mine):
        return jnp.where((row == 3) | (row == 4) | (row >= 6), got, mine)

    def ordered(own, swap, mid, far, c, cc):
        pairs = ((own, swap), (swap, own), (c, mid), (cc, far))
        return jnp.concatenate([jnp.where(end, a, b) for a, b in pairs], axis=1)

    place = jnp.stack([even, left, end, row == 0, row == 1]).astype(jnp.int32)

    lead_own, rest_own, last_own = both(0, block), both(block, raw), both(raw, rows)
    top = test_kernel[:block]
    top, lead_own = tied((top, lead_own))
    given = along_row(jnp.where(even, top[half:], top[:half]), ((0, 1), (1, 0)), ALL_COLS)
    token = jnp.zeros((8, 128), jnp.float32)
    given, rest_own = tied((given, rest_own))

    mine = jnp.where(
        even,
        jnp.concatenate([top[:half], given], axis=0),
        jnp.concatenate([given, top[half:]], axis=0),
    )
    got = near(mine)
    lead_swap = along_col(lead_own, both_ways, most)
    lead_mid = along_col(lead_own, MID_MID, most)
    rest_swap = along_col(rest_own, both_ways, every)
    rest_mid = along_col(rest_own, MID_MID, every)
    token, lead_swap, lead_mid, got, last_own = stage(token, lead_swap, lead_mid, got, last_own)

    mine = near_or(got, mine)
    got = far(mine)
    crossed = lax.ppermute(
        jnp.where(end, last_own, lead_mid), AXES, pairs_of(MID_END, most) + pairs_of(END_MID, every)
    )
    lead_far = along_col(lead_swap, MID_MID, most)
    token, rest_swap, rest_mid, got = stage(token, rest_swap, rest_mid, got)

    mine = far_or(got, mine)
    hop = along_col(mine, END_MID, every)
    rest_far = along_col(rest_swap, MID_MID, every)
    inverses = split_inverses(*tied((first_inverse, second_inverse, token))[:2])
    token, crossed, lead_far = stage(token, crossed, lead_far)

    lead_cc = along_col(lead_far, MID_END, most)
    rest_c = along_col(rest_mid, MID_END, every)
    token, lead_cc = stage(token, lead_cc)

    slabs = [v[:, :slab] for v in (lead_own, lead_swap, lead_mid, lead_far, crossed, lead_cc)]
    corner = ordered(*slabs)
    upper = along_row(corner[:half], ((1, 0),), ALL_COLS)
    corner = jnp.where(even, upper, corner[half:])
    got = near(corner)
    last_sent = jnp.concatenate(tied((last_own, crossed, token))[:2], axis=1)
    last_both = along_col(last_sent, MID_MID, every)
    token, rest_far, hop, got = stage(token, rest_far, hop, got)

    corner = near_or(got, corner)
    got = far(corner)
    rest_cc = along_col(rest_far, MID_END, every)
    hop_other = along_row(hop, SWAP, ALL_COLS)
    token, rest_c, got, hop_other = stage(token, rest_c, got, hop_other)

    corner = far_or(got, corner)
    corner = (corner, along_row(corner, SWAP, ALL_COLS))
    mine, token = tied((mine, token))
    other = along_row(mine, SWAP, ALL_COLS)
    solved_end = solve(place, (hop, hop_other), corner, inverses)
    token, last_both, *solved_end = stage(token, last_both, *solved_end)

    last = (crossed, last_own, last_both)
    sent = multiply(last, solved_end)
    returned = [along_col(value, MID_END, every) for value in sent]
    sent, mine, other = tied((sent, mine, other))

    solved = solve(place, (mine, other), corner, inverses)
    lead = (lead_own, lead_swap, lead_mid, lead_far, crossed, lead_cc)
    out = update_raw(place, test_kernel, solved, lead, 0, True)
    token, rest_cc, out = stage(token, rest_cc, out)

    rest = (rest_own, rest_swap, rest_mid, rest_far, rest_c, rest_cc)
    out = update_raw(place, test_kernel, solved, rest, block, False, out)
    out = update_last(place, test_kernel, last, solved, out)
    for i, value in enumerate(returned):
        out, value = tied((out, value))
        out = finish(place, test_kernel, value, out, raw + (i + 1) * TILE)
    return out


def solution(mesh):
    in_specs = (P("row", "col"), P("row", "col"), P("row", "col"), P(), P())
    out_specs = P("row", "col")
    body = four if dict(mesh.shape) == {"row": ROWS, "col": COLS} else general
    return jax.shard_map(body, mesh=mesh, in_specs=in_specs, out_specs=out_specs, check_vma=False)
```

```python
import functools

import jax
import jax.numpy as jnp
from jax import lax
from jax.experimental import pallas as pl
from jax.experimental.pallas import tpu as pltpu
from jax.sharding import PartitionSpec as P

STAGE_FLOPS = 10**10
FILLERS = 2
STAGE_BYTES = 2**20


def product(left, right):
    return jnp.dot(left, right, precision=lax.Precision.HIGH, preferred_element_type=jnp.float32)


def broadcast(value, axis, source):
    kept = jnp.where(lax.axis_index(axis) == source, value, 0).astype(value.dtype)
    return lax.psum(kept, axis)


def general(test_kernel, first_panel, second_panel, first_inverse, second_inverse):
    block = first_inverse.shape[0]
    position = lax.axis_index("row")
    first_rows = broadcast(test_kernel[:block], "row", 0)
    first_solved = product(first_inverse, first_rows)
    partial_value = test_kernel - product(lax.all_gather(first_panel, "col", axis=1, tiled=True), first_solved)
    second_rows = broadcast(partial_value[:block], "row", 1)
    second_solved = product(second_inverse, second_rows)
    final = partial_value - product(lax.all_gather(second_panel, "col", axis=1, tiled=True), second_solved)
    leading_final = jnp.where(
        position == 0, first_solved, jnp.where(position == 1, second_solved, final[:block])
    )
    return final.at[:block].set(leading_final)


AXES = ("row", "col")
ROWS, COLS = 8, 4
END_MID = ((0, 1), (3, 2))
MID_MID = ((1, 2), (2, 1))
MID_END = ((1, 0), (2, 3))


def pairs_of(pairs, rows):
    return [(r * COLS + a, r * COLS + b) for r in rows for a, b in pairs]


def along_col(value, pairs, rows):
    return lax.ppermute(value, AXES, pairs_of(pairs, rows))


def along_row(value, pairs, cols):
    return lax.ppermute(value, AXES, [(a * COLS + c, b * COLS + c) for a, b in pairs for c in cols])


ALL_COLS = (0, 1, 2, 3)
SWAP = tuple((r, r ^ 1) for r in range(ROWS))


def split(value):
    high = value.astype(jnp.bfloat16)
    return high, (value - high.astype(jnp.float32)).astype(jnp.bfloat16)


def three_pass(left, right):
    def one(a, b):
        return jnp.dot(a, b, preferred_element_type=jnp.float32)

    return one(left[0], right[0]) + (one(left[0], right[1]) + one(left[1], right[0]))


TILE = 256
VMEM_BYTES = 32 * 2**20
SMEM = pl.BlockSpec(memory_space=pltpu.SMEM)


def halves(place, held, other):
    a, b = held[...], other[...]
    return jnp.where(place[0] == 1, a, b), jnp.where(place[0] == 1, b, a)


def solved_tile(place, tops, corners, inverses):
    low, high = halves(place, *tops)
    half = low.shape[0] // 2
    first_top = jnp.concatenate([low[:half], high[:half]], axis=0)
    second_top = jnp.concatenate([low[half:], high[half:]], axis=0)
    corner = jnp.concatenate(halves(place, *corners), axis=0)
    slab = first_top.shape[0] // COLS

    def turned(solved):
        pieces = [solved[k * slab : (k + 1) * slab] for k in range(COLS)]
        return [jnp.where(place[1] == 1, pieces[k], pieces[COLS - 1 - k]) for k in range(COLS)]

    first_high, first_low, second_high, second_low = (ref[...] for ref in inverses)
    first = turned(three_pass((first_high, first_low), split(first_top)))
    value = second_top - three_pass(split(corner), split(jnp.concatenate(first, axis=0)))
    second = turned(three_pass((second_high, second_low), split(value)))
    return jnp.concatenate([p for pair in zip(first, second) for p in pair], axis=0)


def split_kernel(one, two, *outs):
    outs[0][...], outs[1][...] = split(one[...])
    outs[2][...], outs[3][...] = split(two[...])


def split_inverses(one, two):
    return pl.pallas_call(
        split_kernel,
        out_shape=[jax.ShapeDtypeStruct(one.shape, jnp.bfloat16)] * 4,
        compiler_params=pltpu.CompilerParams(vmem_limit_bytes=16 * 2**20),
    )(one, two)


def solve_kernel(place, *refs):
    refs[8][...], refs[9][...] = split(solved_tile(place, refs[:2], refs[2:4], refs[4:8]))


def solve(place, tops, corners, inverses):
    rows, width = 2 * inverses[0].shape[0], tops[0].shape[1]
    part = jax.ShapeDtypeStruct((rows, width), jnp.bfloat16)
    return pl.pallas_call(
        solve_kernel,
        out_shape=[part, part],
        in_specs=[SMEM] + [pl.BlockSpec(memory_space=pltpu.VMEM)] * 8,
        compiler_params=pltpu.CompilerParams(vmem_limit_bytes=VMEM_BYTES),
        cost_estimate=pl.CostEstimate(flops=3 * 10**9, bytes_accessed=0, transcendentals=0),
    )(place, *tops, *corners, *inverses)


def multiply_kernel(near_end, own, both, high, low, *outs):
    panels = jnp.concatenate([near_end[...], own[...], both[...]], axis=1)
    value = three_pass(split(panels), (high[...], low[...]))
    for i, out in enumerate(outs):
        out[...] = value[i * TILE : (i + 1) * TILE]


def multiply(panels, solved):
    rows, width = panels[0].shape[0], solved[0].shape[1]
    return pl.pallas_call(
        multiply_kernel,
        out_shape=[jax.ShapeDtypeStruct((TILE, width), jnp.float32)] * (rows // TILE),
        compiler_params=pltpu.CompilerParams(vmem_limit_bytes=VMEM_BYTES),
        cost_estimate=pl.CostEstimate(flops=2 * 10**9, bytes_accessed=0, transcendentals=0),
    )(*panels, *solved)


def update_raw_kernel(blocks, place, top, high, low, own, swap, mid, far, c, cc, *outs):
    left, end, out = place[1] == 1, place[2] == 1, outs[-1]
    pairs = ((own, swap), (swap, own), (c, mid), (cc, far))
    panels = jnp.concatenate([jnp.where(end, a[...], b[...]) for a, b in pairs], axis=1)
    out[...] = top[...] - three_pass(split(panels), (high[...], low[...]))
    if blocks:
        slab = high.shape[0] // (2 * COLS)
        for which in range(2):
            @pl.when(place[3 + which] == 1)
            def _():
                for k in range(TILE // slab):
                    here = pl.program_id(0) * (TILE // slab) + k
                    here = jnp.where(left, here, COLS - 1 - here)
                    rows = pl.ds(pl.multiple_of((2 * here + which) * slab, slab), slab)
                    value = high[rows].astype(jnp.float32) + low[rows].astype(jnp.float32)
                    out[k * slab : (k + 1) * slab] = value


def update_raw(place, top, solved, group, first, blocks, *out):
    tile = pl.BlockSpec((TILE, top.shape[1]), lambda i: (first // TILE + i, 0))
    part = pl.BlockSpec((TILE, group[0].shape[1]), lambda i: (i, 0))
    return pl.pallas_call(
        functools.partial(update_raw_kernel, blocks),
        grid=(group[0].shape[0] // TILE,),
        out_shape=jax.ShapeDtypeStruct(top.shape, top.dtype),
        in_specs=[SMEM, tile]
        + [pl.BlockSpec(v.shape, lambda i: (0, 0)) for v in solved]
        + [part] * 6
        + [pl.BlockSpec(memory_space=pl.ANY)] * len(out),
        out_specs=tile,
        input_output_aliases={10: 0} if out else {},
        compiler_params=pltpu.CompilerParams(vmem_limit_bytes=VMEM_BYTES),
        cost_estimate=pl.CostEstimate(flops=3 * 10**9, bytes_accessed=0, transcendentals=0),
    )(place, top, *solved, *group, *out)


def update_last_kernel(place, top, near_end, own, both, high, low, kept, out):
    @pl.when(place[2] == 0)
    def _():
        panels = jnp.concatenate([near_end[...], own[...], both[...]], axis=1)
        out[...] = top[...] - three_pass(split(panels), (high[...], low[...]))


def finish_kernel(place, top, returned, kept, out):
    out[...] = jnp.where(place[2] == 1, top[...] - returned[...], kept[...])


def last_call(body, place, top, parts, fixed, out, block_of_out, flops, past):
    width, count = top.shape[1], parts[0].shape[0] // TILE
    first = past // TILE - count
    tile = pl.BlockSpec((TILE, width), lambda i: (first + i, 0))
    return pl.pallas_call(
        body,
        grid=(count,),
        out_shape=jax.ShapeDtypeStruct(top.shape, top.dtype),
        in_specs=[SMEM, tile]
        + [pl.BlockSpec((TILE, v.shape[1]), lambda i: (i, 0)) for v in parts]
        + [pl.BlockSpec(v.shape, lambda i: (0, 0)) for v in fixed]
        + [tile if block_of_out else pl.BlockSpec(memory_space=pl.ANY)],
        out_specs=tile,
        input_output_aliases={2 + len(parts) + len(fixed): 0},
        compiler_params=pltpu.CompilerParams(vmem_limit_bytes=VMEM_BYTES),
        cost_estimate=pl.CostEstimate(flops=flops, bytes_accessed=0, transcendentals=0),
    )(place, top, *parts, *fixed, out)


def update_last(place, top, last, solved, out):
    return last_call(update_last_kernel, place, top, last, solved, out, False, 2 * 10**9, top.shape[0])


def finish(place, top, returned, out, past):
    return last_call(finish_kernel, place, top, (returned,), (), out, True, 10**9, past)


def nothing(*refs):
    pass


def hand_on(*values):
    anywhere = [pl.BlockSpec(memory_space=pl.ANY)] * len(values)
    return pl.pallas_call(
        nothing,
        out_shape=[jax.ShapeDtypeStruct(v.shape, v.dtype) for v in values],
        in_specs=anywhere,
        out_specs=anywhere,
        input_output_aliases={i: i for i in range(len(values))},
        compiler_params=pltpu.CompilerParams(vmem_limit_bytes=STAGE_BYTES),
        cost_estimate=pl.CostEstimate(flops=STAGE_FLOPS, bytes_accessed=0, transcendentals=0),
    )(*values)


def stage(token, *values):
    for _ in range(FILLERS):
        [token] = hand_on(token)
    return hand_on(token, *values)


def four(test_kernel, first_panel, second_panel, first_inverse, second_inverse):
    block = first_inverse.shape[0]
    rows, width = test_kernel.shape
    raw, slab = 3 * block, first_panel.shape[1]
    half = block // 2
    row, col = lax.axis_index("row"), lax.axis_index("col")
    end = (col == 0) | (col == COLS - 1)
    left = col < COLS // 2
    even = row % 2 == 0
    every, most = range(ROWS), range(1, ROWS)
    both_ways = END_MID + MID_END
    tied = lax.optimization_barrier

    def both(low, high):
        return jnp.concatenate([first_panel[low:high], second_panel[low:high]], axis=1)

    def near(mine):
        return along_row(mine, ((0, 2), (1, 5)), ALL_COLS)

    def far(mine):
        return along_row(mine, ((2, 6), (5, 7), (0, 4), (1, 3)), ALL_COLS)

    def near_or(got, mine):
        return jnp.where((row == 2) | (row == 5), got, mine)

    def far_or(got, mine):
        return jnp.where((row == 3) | (row == 4) | (row >= 6), got, mine)

    def ordered(own, swap, mid, far, c, cc):
        pairs = ((own, swap), (swap, own), (c, mid), (cc, far))
        return jnp.concatenate([jnp.where(end, a, b) for a, b in pairs], axis=1)

    place = jnp.stack([even, left, end, row == 0, row == 1]).astype(jnp.int32)

    lead_own, rest_own, last_own = both(0, block), both(block, raw), both(raw, rows)
    top = test_kernel[:block]
    top, lead_own = tied((top, lead_own))
    given = along_row(jnp.where(even, top[half:], top[:half]), ((0, 1), (1, 0)), ALL_COLS)
    token = jnp.zeros((8, 128), jnp.float32)
    given, rest_own = tied((given, rest_own))

    mine = jnp.where(
        even,
        jnp.concatenate([top[:half], given], axis=0),
        jnp.concatenate([given, top[half:]], axis=0),
    )
    got = near(mine)
    lead_swap = along_col(lead_own, both_ways, most)
    lead_mid = along_col(lead_own, MID_MID, most)
    rest_swap = along_col(rest_own, both_ways, every)
    rest_mid = along_col(rest_own, MID_MID, every)
    token, lead_swap, lead_mid, got, last_own = stage(token, lead_swap, lead_mid, got, last_own)

    mine = near_or(got, mine)
    got = far(mine)
    crossed = lax.ppermute(
        jnp.where(end, last_own, lead_mid), AXES, pairs_of(MID_END, most) + pairs_of(END_MID, every)
    )
    lead_far = along_col(lead_swap, MID_MID, most)
    token, rest_swap, rest_mid, got = stage(token, rest_swap, rest_mid, got)

    mine = far_or(got, mine)
    hop = along_col(mine, END_MID, every)
    rest_far = along_col(rest_swap, MID_MID, every)
    inverses = split_inverses(*tied((first_inverse, second_inverse, token))[:2])
    token, lead_far = stage(token, lead_far)

    lead_cc = along_col(lead_far, MID_END, most)
    rest_c = along_col(rest_mid, MID_END, every)
    token, lead_cc, crossed = stage(token, lead_cc, crossed)

    slabs = [v[:, :slab] for v in (lead_own, lead_swap, lead_mid, lead_far, crossed, lead_cc)]
    corner = ordered(*slabs)
    upper = along_row(corner[:half], ((1, 0),), ALL_COLS)
    corner = jnp.where(even, upper, corner[half:])
    got = near(corner)
    last_sent = jnp.concatenate(tied((last_own, crossed, token))[:2], axis=1)
    last_both = along_col(last_sent, MID_MID, every)
    token, rest_far, hop, got = stage(token, rest_far, hop, got)

    corner = near_or(got, corner)
    got = far(corner)
    rest_cc = along_col(rest_far, MID_END, every)
    hop_other = along_row(hop, SWAP, ALL_COLS)
    token, rest_c, got, hop_other = stage(token, rest_c, got, hop_other)

    corner = far_or(got, corner)
    corner = (corner, along_row(corner, SWAP, ALL_COLS))
    mine, token = tied((mine, token))
    other = along_row(mine, SWAP, ALL_COLS)
    solved_end = solve(place, (hop, hop_other), corner, inverses)
    token, last_both, *solved_end = stage(token, last_both, *solved_end)

    last = (crossed, last_own, last_both)
    sent = multiply(last, solved_end)
    returned = [along_col(value, MID_END, every) for value in sent]
    sent, mine, other = tied((sent, mine, other))

    solved = solve(place, (mine, other), corner, inverses)
    lead = (lead_own, lead_swap, lead_mid, lead_far, crossed, lead_cc)
    out = update_raw(place, test_kernel, solved, lead, 0, True)
    token, rest_cc, out = stage(token, rest_cc, out)

    rest = (rest_own, rest_swap, rest_mid, rest_far, rest_c, rest_cc)
    out = update_raw(place, test_kernel, solved, rest, block, False, out)
    out = update_last(place, test_kernel, last, solved, out)
    for i, value in enumerate(returned):
        out, value = tied((out, value))
        out = finish(place, test_kernel, value, out, raw + (i + 1) * TILE)
    return out


def solution(mesh):
    in_specs = (P("row", "col"), P("row", "col"), P("row", "col"), P(), P())
    out_specs = P("row", "col")
    body = four if dict(mesh.shape) == {"row": ROWS, "col": COLS} else general
    return jax.shard_map(body, mesh=mesh, in_specs=in_specs, out_specs=out_specs, check_vma=False)
```

```python
import functools

import jax
import jax.numpy as jnp
from jax import lax
from jax.experimental import pallas as pl
from jax.experimental.pallas import tpu as pltpu
from jax.sharding import PartitionSpec as P

STAGE_FLOPS = 10**10
FILLERS = 2
STAGE_BYTES = 2**20


def product(left, right):
    return jnp.dot(left, right, precision=lax.Precision.HIGH, preferred_element_type=jnp.float32)


def broadcast(value, axis, source):
    kept = jnp.where(lax.axis_index(axis) == source, value, 0).astype(value.dtype)
    return lax.psum(kept, axis)


def general(test_kernel, first_panel, second_panel, first_inverse, second_inverse):
    block = first_inverse.shape[0]
    position = lax.axis_index("row")
    first_rows = broadcast(test_kernel[:block], "row", 0)
    first_solved = product(first_inverse, first_rows)
    partial_value = test_kernel - product(lax.all_gather(first_panel, "col", axis=1, tiled=True), first_solved)
    second_rows = broadcast(partial_value[:block], "row", 1)
    second_solved = product(second_inverse, second_rows)
    final = partial_value - product(lax.all_gather(second_panel, "col", axis=1, tiled=True), second_solved)
    leading_final = jnp.where(
        position == 0, first_solved, jnp.where(position == 1, second_solved, final[:block])
    )
    return final.at[:block].set(leading_final)


AXES = ("row", "col")
ROWS, COLS = 8, 4
END_MID = ((0, 1), (3, 2))
MID_MID = ((1, 2), (2, 1))
MID_END = ((1, 0), (2, 3))


def pairs_of(pairs, rows):
    return [(r * COLS + a, r * COLS + b) for r in rows for a, b in pairs]


def along_col(value, pairs, rows):
    return lax.ppermute(value, AXES, pairs_of(pairs, rows))


def along_row(value, pairs, cols):
    return lax.ppermute(value, AXES, [(a * COLS + c, b * COLS + c) for a, b in pairs for c in cols])


ALL_COLS = (0, 1, 2, 3)
SWAP = tuple((r, r ^ 1) for r in range(ROWS))


def split(value):
    high = value.astype(jnp.bfloat16)
    return high, (value - high.astype(jnp.float32)).astype(jnp.bfloat16)


def three_pass(left, right):
    def one(a, b):
        return jnp.dot(a, b, preferred_element_type=jnp.float32)

    return one(left[0], right[0]) + (one(left[0], right[1]) + one(left[1], right[0]))


TILE, SHORT = 256, 128
VMEM_BYTES = 32 * 2**20
SMEM = pl.BlockSpec(memory_space=pltpu.SMEM)


def halves(place, held, other):
    a, b = held[...], other[...]
    return jnp.where(place[0] == 1, a, b), jnp.where(place[0] == 1, b, a)


def solved_tile(place, tops, corners, inverses):
    low, high = halves(place, *tops)
    half = low.shape[0] // 2
    first_top = jnp.concatenate([low[:half], high[:half]], axis=0)
    second_top = jnp.concatenate([low[half:], high[half:]], axis=0)
    corner = jnp.concatenate(halves(place, *corners), axis=0)
    slab = first_top.shape[0] // COLS

    def turned(solved):
        pieces = [solved[k * slab : (k + 1) * slab] for k in range(COLS)]
        return [jnp.where(place[1] == 1, pieces[k], pieces[COLS - 1 - k]) for k in range(COLS)]

    first_high, first_low, second_high, second_low = (ref[...] for ref in inverses)
    first = turned(three_pass((first_high, first_low), split(first_top)))
    value = second_top - three_pass(split(corner), split(jnp.concatenate(first, axis=0)))
    second = turned(three_pass((second_high, second_low), split(value)))
    return jnp.concatenate([p for pair in zip(first, second) for p in pair], axis=0)


def split_kernel(one, two, *outs):
    outs[0][...], outs[1][...] = split(one[...])
    outs[2][...], outs[3][...] = split(two[...])


def split_inverses(one, two):
    return pl.pallas_call(
        split_kernel,
        out_shape=[jax.ShapeDtypeStruct(one.shape, jnp.bfloat16)] * 4,
        compiler_params=pltpu.CompilerParams(vmem_limit_bytes=16 * 2**20),
    )(one, two)


def solve_kernel(place, *refs):
    refs[8][...], refs[9][...] = split(solved_tile(place, refs[:2], refs[2:4], refs[4:8]))


def solve(place, tops, corners, inverses):
    rows, width = 2 * inverses[0].shape[0], tops[0].shape[1]
    part = jax.ShapeDtypeStruct((rows, width), jnp.bfloat16)
    return pl.pallas_call(
        solve_kernel,
        out_shape=[part, part],
        in_specs=[SMEM] + [pl.BlockSpec(memory_space=pltpu.VMEM)] * 8,
        compiler_params=pltpu.CompilerParams(vmem_limit_bytes=VMEM_BYTES),
        cost_estimate=pl.CostEstimate(flops=3 * 10**9, bytes_accessed=0, transcendentals=0),
    )(place, *tops, *corners, *inverses)


def multiply_kernel(near_end, own, both, high, low, *outs):
    panels = jnp.concatenate([near_end[...], own[...], both[...]], axis=1)
    value = three_pass(split(panels), (high[...], low[...]))
    outs[0][...], outs[1][...] = value[:-SHORT], value[-SHORT:]


def multiply(panels, solved):
    rows, width = panels[0].shape[0], solved[0].shape[1]
    return pl.pallas_call(
        multiply_kernel,
        out_shape=[jax.ShapeDtypeStruct((n, width), jnp.float32) for n in (rows - SHORT, SHORT)],
        compiler_params=pltpu.CompilerParams(vmem_limit_bytes=VMEM_BYTES),
        cost_estimate=pl.CostEstimate(flops=2 * 10**9, bytes_accessed=0, transcendentals=0),
    )(*panels, *solved)


def update_raw_kernel(blocks, place, top, high, low, own, swap, mid, far, c, cc, *outs):
    left, end, out = place[1] == 1, place[2] == 1, outs[-1]
    pairs = ((own, swap), (swap, own), (c, mid), (cc, far))
    panels = jnp.concatenate([jnp.where(end, a[...], b[...]) for a, b in pairs], axis=1)
    out[...] = top[...] - three_pass(split(panels), (high[...], low[...]))
    if blocks:
        slab = high.shape[0] // (2 * COLS)
        for which in range(2):
            @pl.when(place[3 + which] == 1)
            def _():
                for k in range(TILE // slab):
                    here = pl.program_id(0) * (TILE // slab) + k
                    here = jnp.where(left, here, COLS - 1 - here)
                    rows = pl.ds(pl.multiple_of((2 * here + which) * slab, slab), slab)
                    value = high[rows].astype(jnp.float32) + low[rows].astype(jnp.float32)
                    out[k * slab : (k + 1) * slab] = value


def update_raw(place, top, solved, group, first, blocks, *out):
    tile = pl.BlockSpec((TILE, top.shape[1]), lambda i: (first // TILE + i, 0))
    part = pl.BlockSpec((TILE, group[0].shape[1]), lambda i: (i, 0))
    return pl.pallas_call(
        functools.partial(update_raw_kernel, blocks),
        grid=(group[0].shape[0] // TILE,),
        out_shape=jax.ShapeDtypeStruct(top.shape, top.dtype),
        in_specs=[SMEM, tile]
        + [pl.BlockSpec(v.shape, lambda i: (0, 0)) for v in solved]
        + [part] * 6
        + [pl.BlockSpec(memory_space=pl.ANY)] * len(out),
        out_specs=tile,
        input_output_aliases={10: 0} if out else {},
        compiler_params=pltpu.CompilerParams(vmem_limit_bytes=VMEM_BYTES),
        cost_estimate=pl.CostEstimate(flops=3 * 10**9, bytes_accessed=0, transcendentals=0),
    )(place, top, *solved, *group, *out)


def update_last_kernel(place, top, near_end, own, both, high, low, kept, out):
    @pl.when(place[2] == 0)
    def _():
        panels = jnp.concatenate([near_end[...], own[...], both[...]], axis=1)
        out[...] = top[...] - three_pass(split(panels), (high[...], low[...]))


def finish_kernel(place, top, returned, kept, out):
    out[...] = jnp.where(place[2] == 1, top[...] - returned[...], kept[...])


def last_call(body, place, top, parts, fixed, out, block_of_out, flops, past):
    step = SHORT if parts[0].shape[0] % TILE else TILE
    width, count = top.shape[1], parts[0].shape[0] // step
    first = past // step - count
    tile = pl.BlockSpec((step, width), lambda i: (first + i, 0))
    return pl.pallas_call(
        body,
        grid=(count,),
        out_shape=jax.ShapeDtypeStruct(top.shape, top.dtype),
        in_specs=[SMEM, tile]
        + [pl.BlockSpec((step, v.shape[1]), lambda i: (i, 0)) for v in parts]
        + [pl.BlockSpec(v.shape, lambda i: (0, 0)) for v in fixed]
        + [tile if block_of_out else pl.BlockSpec(memory_space=pl.ANY)],
        out_specs=tile,
        input_output_aliases={2 + len(parts) + len(fixed): 0},
        compiler_params=pltpu.CompilerParams(vmem_limit_bytes=VMEM_BYTES),
        cost_estimate=pl.CostEstimate(flops=flops, bytes_accessed=0, transcendentals=0),
    )(place, top, *parts, *fixed, out)


def update_last(place, top, last, solved, out):
    return last_call(update_last_kernel, place, top, last, solved, out, False, 2 * 10**9, top.shape[0])


def finish(place, top, returned, out, past):
    return last_call(finish_kernel, place, top, (returned,), (), out, True, 10**9, past)


def nothing(*refs):
    pass


def hand_on(*values):
    anywhere = [pl.BlockSpec(memory_space=pl.ANY)] * len(values)
    return pl.pallas_call(
        nothing,
        out_shape=[jax.ShapeDtypeStruct(v.shape, v.dtype) for v in values],
        in_specs=anywhere,
        out_specs=anywhere,
        input_output_aliases={i: i for i in range(len(values))},
        compiler_params=pltpu.CompilerParams(vmem_limit_bytes=STAGE_BYTES),
        cost_estimate=pl.CostEstimate(flops=STAGE_FLOPS, bytes_accessed=0, transcendentals=0),
    )(*values)


def stage(token, *values):
    for _ in range(FILLERS):
        [token] = hand_on(token)
    return hand_on(token, *values)


def four(test_kernel, first_panel, second_panel, first_inverse, second_inverse):
    block = first_inverse.shape[0]
    rows, width = test_kernel.shape
    raw, slab = 3 * block, first_panel.shape[1]
    half = block // 2
    row, col = lax.axis_index("row"), lax.axis_index("col")
    end = (col == 0) | (col == COLS - 1)
    left = col < COLS // 2
    even = row % 2 == 0
    every, most = range(ROWS), range(1, ROWS)
    both_ways = END_MID + MID_END
    tied = lax.optimization_barrier

    def both(low, high):
        return jnp.concatenate([first_panel[low:high], second_panel[low:high]], axis=1)

    def near(mine):
        return along_row(mine, ((0, 2), (1, 5)), ALL_COLS)

    def far(mine):
        return along_row(mine, ((2, 6), (5, 7), (0, 4), (1, 3)), ALL_COLS)

    def near_or(got, mine):
        return jnp.where((row == 2) | (row == 5), got, mine)

    def far_or(got, mine):
        return jnp.where((row == 3) | (row == 4) | (row >= 6), got, mine)

    def ordered(own, swap, mid, far, c, cc):
        pairs = ((own, swap), (swap, own), (c, mid), (cc, far))
        return jnp.concatenate([jnp.where(end, a, b) for a, b in pairs], axis=1)

    place = jnp.stack([even, left, end, row == 0, row == 1]).astype(jnp.int32)

    lead_own, rest_own, last_own = both(0, block), both(block, raw), both(raw, rows)
    top = test_kernel[:block]
    top, lead_own = tied((top, lead_own))
    given = along_row(jnp.where(even, top[half:], top[:half]), ((0, 1), (1, 0)), ALL_COLS)
    token = jnp.zeros((8, 128), jnp.float32)
    given, rest_own = tied((given, rest_own))

    mine = jnp.where(
        even,
        jnp.concatenate([top[:half], given], axis=0),
        jnp.concatenate([given, top[half:]], axis=0),
    )
    got = near(mine)
    lead_swap = along_col(lead_own, both_ways, most)
    lead_mid = along_col(lead_own, MID_MID, most)
    rest_swap = along_col(rest_own, both_ways, every)
    rest_mid = along_col(rest_own, MID_MID, every)
    token, lead_swap, lead_mid, got, last_own = stage(token, lead_swap, lead_mid, got, last_own)

    mine = near_or(got, mine)
    got = far(mine)
    crossed = lax.ppermute(
        jnp.where(end, last_own, lead_mid), AXES, pairs_of(MID_END, most) + pairs_of(END_MID, every)
    )
    lead_far = along_col(lead_swap, MID_MID, most)
    token, rest_swap, rest_mid, got = stage(token, rest_swap, rest_mid, got)

    mine = far_or(got, mine)
    hop = along_col(mine, END_MID, every)
    rest_far = along_col(rest_swap, MID_MID, every)
    inverses = split_inverses(*tied((first_inverse, second_inverse, token))[:2])
    token, lead_far = stage(token, lead_far)

    lead_cc = along_col(lead_far, MID_END, most)
    rest_c = along_col(rest_mid, MID_END, every)
    token, lead_cc, crossed = stage(token, lead_cc, crossed)

    slabs = [v[:, :slab] for v in (lead_own, lead_swap, lead_mid, lead_far, crossed, lead_cc)]
    corner = ordered(*slabs)
    upper = along_row(corner[:half], ((1, 0),), ALL_COLS)
    corner = jnp.where(even, upper, corner[half:])
    got = near(corner)
    last_sent = jnp.concatenate(tied((last_own, crossed, token))[:2], axis=1)
    last_both = along_col(last_sent, MID_MID, every)
    token, rest_far, hop, got = stage(token, rest_far, hop, got)

    corner = near_or(got, corner)
    got = far(corner)
    rest_cc = along_col(rest_far, MID_END, every)
    hop_other = along_row(hop, SWAP, ALL_COLS)
    token, rest_c, got, hop_other = stage(token, rest_c, got, hop_other)

    corner = far_or(got, corner)
    corner = (corner, along_row(corner, SWAP, ALL_COLS))
    mine, token = tied((mine, token))
    other = along_row(mine, SWAP, ALL_COLS)
    solved_end = solve(place, (hop, hop_other), corner, inverses)
    token, last_both, *solved_end = stage(token, last_both, *solved_end)

    last = (crossed, last_own, last_both)
    sent = multiply(last, solved_end)
    returned = [along_col(value, MID_END, every) for value in sent]
    sent, mine, other = tied((sent, mine, other))

    solved = solve(place, (mine, other), corner, inverses)
    lead = (lead_own, lead_swap, lead_mid, lead_far, crossed, lead_cc)
    out = update_raw(place, test_kernel, solved, lead, 0, True)
    token, rest_cc, out = stage(token, rest_cc, out)

    rest = (rest_own, rest_swap, rest_mid, rest_far, rest_c, rest_cc)
    out = update_raw(place, test_kernel, solved, rest, block, False, out)
    out = update_last(place, test_kernel, last, solved, out)
    for past, value in zip((rows - SHORT, rows), returned):
        out, value = tied((out, value))
        out = finish(place, test_kernel, value, out, past)
    return out


def solution(mesh):
    in_specs = (P("row", "col"), P("row", "col"), P("row", "col"), P(), P())
    out_specs = P("row", "col")
    body = four if dict(mesh.shape) == {"row": ROWS, "col": COLS} else general
    return jax.shard_map(body, mesh=mesh, in_specs=in_specs, out_specs=out_specs, check_vma=False)
```
